32 devices in a mesh: grp: 2 (over y), wide: 16 (over z, x, core).
Axes of the slice: x: 2, y: 2, z: 4, core: 2. Of those that a mesh axis runs over, the one named last changes fastest.
Arguments:
- coeff: float32 [256, 6144], P(('grp', 'wide')), may hold values from -6 to 6
- beta_blocks: float32 [96, 128, 128], replicated, may hold values from -0.5 to 0.5
- block_list: int32 [2, 96], replicated, may hold values from 0 to 47
- alpha_blocks: float32 [32, 2, 8, 8], P(('grp', 'wide')), may hold values from -2 to 2
- partner_mask: int32 [32, 2], P(('grp', 'wide')), may hold values 0 or 1
- exc_source: int32 [90, 256], P(None, 'grp'), may hold values from 0 to 255
- exc_pair: int32 [90, 256], P(None, 'grp'), may hold values from 0 to 323
- exc_parity: int32 [90, 256], P(None, 'grp'), may hold values from 0 to 1
- occupation: int32 [18, 6144], P(None, 'wide'), may hold values 0 or 1
- coulomb: float32 [324, 18], replicated, may hold values from -0.2 to 0.2
Outputs:
- sigma: float32 [256, 6144], P(('grp', 'wide'))
The draws below stay inside these ranges and needn't reach their ends.
Inputs may be any that keep to these rules, and one draw needn't show every extreme that they name: `exc_source`: any alpha string.
All inputs are finite; a program needn't handle non-finite values. No bound on the sum of `partner_mask` or of `occupation` on one device may be relied on, other than what follows from the above.
Results may differ from the reference program's by a relative error of at most 0.0003.
Values sent between devices are 32-bit elements; how exact they have to be, the bound alone decides.
A program may use at most 128 MiB of HBM per device.

```python
import jax
import jax.numpy as jnp
from jax import lax

RA = 8
NB = 6144
SB = 128
P_SIZE = 96
NORB = 18
NEXC = 90
NPAIR = 324
NBB = 48
ABLK = 32
NA = 256
N_GRP = 2
N_WIDE = 16


def place_ends(result, stream_key, least, top_value):
    dims = result.shape
    place = [jax.random.randint(jax.random.fold_in(stream_key, axis), (), 0, dims[axis]) for axis in range(len(dims))]
    result = result.at[tuple(place)].set(least)
    longest = dims.index(max(dims))
    place[longest] = (place[longest] + 1) % dims[longest]
    return result.at[tuple(place)].set(top_value)


def block_levels(key, dims, shards, smallest, top_value):
    level = 1.0
    for dim, blocks in shards:
        draws = jax.random.uniform(jax.random.fold_in(jax.random.fold_in(key, 6), dim), (blocks,), jnp.float32, smallest / len(shards), top_value / len(shards))
        level = level * jnp.repeat(jnp.exp(draws), dims[dim] // blocks).reshape((-1,) + (1,) * (len(dims) - 1 - dim))
    return level


def bell_draw(stream_key, shape, deviation, limit, cuts=(), dtype=jnp.bfloat16):
    result = jax.random.normal(stream_key, shape, jnp.float32) * deviation
    if len(cuts) > 0:
        result = block_levels(stream_key, shape, cuts, -0.22, 0.18) * result
    return jnp.clip(result, min=-limit, max=limit).astype(dtype)


def setup_inputs(seed: int = 0) -> dict:
    keys = jax.random.split(jax.random.key(seed), 11)
    coeff = bell_draw(keys[0], (NA, NB), 1.0, 6.0, ((0, 32),), jnp.float32)
    beta_blocks = bell_draw(keys[1], (P_SIZE, SB, SB), SB ** -0.5, 0.5, (), jnp.float32)
    block_list = place_ends(jax.random.randint(keys[2], (2, P_SIZE), 0, NBB), jax.random.fold_in(keys[2], 1), 0, NBB - 1).astype(jnp.int32)
    alpha_blocks = bell_draw(keys[3], (ABLK, N_GRP, RA, RA), RA ** -0.5, 2.0, ((0, 32),), jnp.float32)
    partner_mask = place_ends((jax.random.randint(keys[4], (ABLK, N_GRP), 0, 3) < 2).astype(jnp.int32), jax.random.fold_in(keys[4], 1), 0, 1)
    exc_source = place_ends(jax.random.randint(keys[5], (NEXC, NA), 0, NA), jax.random.fold_in(keys[5], 1), 0, NA - 1).astype(jnp.int32)
    exc_pair = place_ends(jax.random.randint(keys[6], (NEXC, NA), 0, NPAIR), jax.random.fold_in(keys[6], 1), 0, NPAIR - 1).astype(jnp.int32)
    exc_parity = place_ends(jax.random.randint(keys[7], (NEXC, NA), 0, 2), jax.random.fold_in(keys[7], 1), 0, 1).astype(jnp.int32)
    occupation = place_ends((jax.random.randint(keys[8], (NORB, NB), 0, 2) < 1).astype(jnp.int32), jax.random.fold_in(keys[8], 1), 0, 1)
    coulomb = bell_draw(keys[9], (NPAIR, NORB), 0.035, 0.2, (), jnp.float32)
    return {"coeff": coeff, "beta_blocks": beta_blocks, "block_list": block_list, "alpha_blocks": alpha_blocks, "partner_mask": partner_mask, "exc_source": exc_source, "exc_pair": exc_pair, "exc_parity": exc_parity, "occupation": occupation, "coulomb": coulomb}


HIGH = lax.Precision.HIGHEST


def reference(coeff, beta_blocks, block_list, alpha_blocks, partner_mask, exc_source, exc_pair, exc_parity, occupation, coulomb):
    blocked = coeff.reshape(NA, NBB, SB)

    def add_block(index, accum):
        source = block_list[0, index].astype(jnp.int32)
        target = block_list[1, index].astype(jnp.int32)
        column = lax.dynamic_index_in_dim(blocked, source, 1, keepdims=False)
        term = jnp.dot(column, beta_blocks[index], precision=HIGH, preferred_element_type=jnp.float32)
        before = lax.dynamic_index_in_dim(accum, target, 1, keepdims=False)
        return lax.dynamic_update_index_in_dim(accum, before + term, target, 1)

    same_beta = lax.fori_loop(0, P_SIZE, add_block, jnp.zeros((NA, NBB, SB), jnp.float32)).reshape(NA, NB)

    grouped = coeff.reshape(N_GRP, N_WIDE, RA, NB)
    masked = alpha_blocks.reshape(N_GRP, N_WIDE, N_GRP, RA, RA) * partner_mask.reshape(N_GRP, N_WIDE, N_GRP)[:, :, :, None, None].astype(jnp.float32)
    same_alpha = jnp.einsum("gwhrs,hwsn->gwrn", masked, grouped, precision=HIGH).reshape(NA, NB)

    weights = jnp.dot(coulomb, occupation.astype(jnp.float32), precision=HIGH, preferred_element_type=jnp.float32)

    def add_single(accum, entry):
        source, pair_row, parity = entry
        fetched = jnp.take(coeff, source.astype(jnp.int32), axis=0)
        factor = jnp.take(weights, pair_row.astype(jnp.int32), axis=0)
        phase = 1.0 - 2.0 * parity.astype(jnp.float32)
        return accum + phase[:, None] * factor * fetched, None

    mixed, _ = lax.scan(add_single, jnp.zeros((NA, NB), jnp.float32), (exc_source, exc_pair, exc_parity))
    return same_beta + same_alpha + mixed
```

```python
import functools

import jax
import jax.numpy as jnp
from jax import lax
from jax.experimental import pallas as pl
from jax.experimental.pallas import tpu as pltpu
from jax.sharding import PartitionSpec as P

HIGH = lax.Precision.HIGHEST
LANES = 128
MESH = pl.DeviceIdType.MESH
F32 = jnp.float32
BF16 = jnp.bfloat16


def split_two(x):
    high = x.astype(BF16).astype(F32)
    return high, x - high


def kernel(
    n_grp,
    n_wide,
    n_orb,
    coeff,
    beta,
    blocks,
    alpha,
    mask,
    source,
    pair,
    parity,
    occupation,
    coulomb,
    out,
    strings,
    strings_high,
    strings_low,
    partner,
    staged,
    arrived,
    dense,
    picked_high,
    picked_low,
    applied,
    placed,
    padded,
    source_t,
    pair_t,
    sign_t,
    wide_c,
    table,
    occ,
    left,
    onehot,
    m_high,
    m_low,
    beta_sem,
    go_send,
    go_recv,
    relay_send,
    relay_recv,
    back_send,
    back_recv,
    partner_send,
    partner_recv,
):
    g = lax.axis_index("grp")
    w = lax.axis_index("wide")
    rows, width = coeff.shape
    cut = width // n_wide
    exc = source.shape[0]
    n_pair = coulomb.shape[0]
    chunks = table.shape[1] // LANES
    n_strings = n_grp * n_wide * rows
    k_size = rows * LANES
    p_size = blocks.shape[1]
    size = beta.shape[1]
    n_blocks = width // size

    barrier = pltpu.get_barrier_semaphore()

    def greet(d, _):
        pl.semaphore_signal(
            barrier, inc=1, device_id=(g, lax.rem(w + d, n_wide)), device_id_type=MESH
        )
        return 0

    lax.fori_loop(1, n_wide, greet, 0)
    for h in range(1, n_grp):
        pl.semaphore_signal(
            barrier, inc=1, device_id=(lax.rem(g + h, n_grp), w), device_id_type=MESH
        )
    fetch = pltpu.make_async_copy(beta, dense, beta_sem)
    fetch.start()
    pl.semaphore_wait(barrier, n_wide - 1 + n_grp - 1)

    def columns(j):
        return pl.ds(pl.multiple_of(j * cut, LANES), cut)

    def go(d):
        to = lax.rem(w + d, n_wide)
        return pltpu.make_async_remote_copy(
            src_ref=coeff.at[:, columns(to)],
            dst_ref=strings.at[g * n_wide + w],
            send_sem=go_send.at[d],
            recv_sem=go_recv.at[d],
            device_id=(g, to),
            device_id_type=MESH,
        )

    def relay(d, h):
        slot = g * n_wide + lax.rem(w - d + n_wide, n_wide)
        return pltpu.make_async_remote_copy(
            src_ref=strings.at[slot],
            dst_ref=strings.at[slot],
            send_sem=relay_send.at[h, d],
            recv_sem=relay_recv.at[h, d],
            device_id=(lax.rem(g + h, n_grp), w),
            device_id_type=MESH,
        )

    def back(d):
        to = lax.rem(w + d, n_wide)
        return pltpu.make_async_remote_copy(
            src_ref=staged.at[to],
            dst_ref=arrived.at[w],
            send_sem=back_send.at[d],
            recv_sem=back_recv.at[d],
            device_id=(g, to),
            device_id_type=MESH,
        )

    def across(h):
        return pltpu.make_async_remote_copy(
            src_ref=coeff,
            dst_ref=partner.at[g],
            send_sem=partner_send.at[h],
            recv_sem=partner_recv.at[h],
            device_id=(lax.rem(g + h, n_grp), w),
            device_id_type=MESH,
        )

    def start_go(d, _):
        go(d).start()
        return 0

    lax.fori_loop(1, n_wide, start_go, 0)
    strings[g * n_wide + w] = coeff[:, columns(w)]
    for h in range(1, n_grp):
        relay(0, h).start()

    padded[...] = jnp.zeros_like(padded)
    padded[0:exc, :] = source[...]
    source_t[...] = padded[...].T
    padded[0:exc, :] = pair[...]
    pair_t[...] = padded[...].T
    padded[0:exc, :] = 1 - 2 * parity[...]
    sign_t[...] = padded[...].T.astype(F32)
    wide_c[...] = jnp.zeros_like(wide_c)
    wide_c[0:n_pair, 0:n_orb] = coulomb[...]
    for c in range(chunks):
        table[:, c * LANES : (c + 1) * LANES] = wide_c[c * LANES : (c + 1) * LANES, :].T
    for r in range(n_orb):
        occ[r] = jnp.broadcast_to(occupation[r : r + 1, :].astype(F32), (rows, cut))

    def build(block):
        at = pl.ds(pl.multiple_of(block * rows, rows), rows)
        pairs = pair_t[at, :]
        signs = sign_t[at, :]
        which = pairs // LANES
        lane = pairs - which * LANES
        sublane = lax.broadcasted_iota(jnp.int32, (rows, LANES), 0)
        for r in range(0, n_orb, 2):
            halves = []
            for q in (r, r + 1):
                value = jnp.zeros((rows, LANES), F32)
                for c in range(chunks):
                    line = jnp.broadcast_to(
                        table[q : q + 1, c * LANES : (c + 1) * LANES], (rows, LANES)
                    )
                    got = jnp.take_along_axis(line, lane, axis=1, mode="promise_in_bounds")
                    value = jnp.where(which == c, got, value)
                halves.append(split_two(value * signs))
            for part in range(2):
                base = part * n_orb * rows + r * rows
                for a in range(rows):
                    both = jnp.concatenate(
                        [jnp.where(sublane == a, half[part], 0.0) for half in halves], axis=0
                    )
                    left[base : base + 2 * rows, a * LANES : (a + 1) * LANES] = both.astype(BF16)
        string = lax.broadcasted_iota(jnp.int32, (n_strings, LANES), 0)
        sources = source_t[at, :]
        for a in range(rows):
            hit = string == jnp.broadcast_to(sources[a : a + 1, :], (n_strings, LANES))
            onehot[:, a * LANES : (a + 1) * LANES] = jnp.where(hit, 1.0, 0.0).astype(BF16)
        m = lax.dot_general(
            left[...], onehot[...], (((1,), (1,)), ((), ())), preferred_element_type=F32
        )
        m = m[: n_orb * rows] + m[n_orb * rows :]
        high, low = split_two(m)
        m_high[block] = high.astype(BF16)
        m_low[block] = low.astype(BF16)

    build(0)

    def build_and_relay(d, _):
        build(d)
        go(d).wait_recv()
        for h in range(1, n_grp):
            relay(d, h).start()
        return 0

    lax.fori_loop(1, n_wide, build_and_relay, 0)
    for h in range(1, n_grp):
        across(h).start()

    def wait_relay(d, _):
        for h in range(1, n_grp):
            relay(d, h).wait_recv()
        return 0

    lax.fori_loop(0, n_wide, wait_relay, 0)
    high, low = split_two(strings[...].reshape(n_strings, cut))
    strings_high[...] = high.astype(BF16)
    strings_low[...] = low.astype(BF16)

    def mix(to):
        y = jnp.dot(m_high[to], strings_high[...], preferred_element_type=F32)
        y += jnp.dot(m_low[to], strings_high[...], preferred_element_type=F32)
        y += jnp.dot(m_high[to], strings_low[...], preferred_element_type=F32)
        total = y[0:rows] * occ[0]
        for r in range(1, n_orb):
            total += y[r * rows : (r + 1) * rows] * occ[r]
        return total

    def mix_and_send(d, _):
        to = lax.rem(w + d, n_wide)
        staged[to] = mix(to)
        back(d).start()
        return 0

    lax.fori_loop(1, n_wide, mix_and_send, 0)
    arrived[w] = mix(w)

    fetch.wait()

    for t in range(n_blocks):
        placed[t * rows : (t + 1) * rows, :] = coeff[:, t * size : (t + 1) * size]
    source_hit = lax.broadcasted_iota(jnp.int32, (p_size, n_blocks), 1) == jnp.broadcast_to(
        blocks_column(blocks, p_size), (p_size, n_blocks)
    )
    choose = jnp.where(source_hit, 1.0, 0.0).astype(BF16)
    for r in range(rows):
        high, low = split_two(placed[pl.ds(r, n_blocks, stride=rows), :])
        picked_high[pl.ds(r, p_size, stride=rows), :] = jnp.dot(
            choose, high.astype(BF16), preferred_element_type=F32
        )
        picked_low[pl.ds(r, p_size, stride=rows), :] = jnp.dot(
            choose, low.astype(BF16), preferred_element_type=F32
        )

    def pick(k):
        at = pl.ds(pl.multiple_of(k * rows, rows), rows)
        high, low = picked_high[at, :], picked_low[at, :]
        return jnp.concatenate(
            [
                jnp.concatenate([high, high], axis=1),
                jnp.concatenate([low, jnp.zeros_like(low)], axis=1),
            ],
            axis=0,
        )

    def apply_two(i, _):
        k = 2 * i
        lhs = jnp.concatenate([pick(k), pick(k + 1)], axis=0).astype(BF16)
        h0, l0 = split_two(dense[k])
        h1, l1 = split_two(dense[k + 1])
        rhs = jnp.concatenate(
            [jnp.concatenate([h0, h1], axis=1), jnp.concatenate([l0, l1], axis=1)], axis=0
        ).astype(BF16)
        y = jnp.dot(lhs, rhs, preferred_element_type=F32)
        applied[pl.ds(k, rows, stride=p_size), :] = y[0:rows, :size] + y[rows : 2 * rows, :size]
        applied[pl.ds(k + 1, rows, stride=p_size), :] = (
            y[2 * rows : 3 * rows, size:] + y[3 * rows :, size:]
        )
        return 0

    lax.fori_loop(0, p_size // 2, apply_two, 0)

    target = jnp.broadcast_to(blocks_row(blocks, p_size), (n_blocks, p_size))
    place = jnp.where(
        lax.broadcasted_iota(jnp.int32, (n_blocks, p_size), 0) == target, 1.0, 0.0
    ).astype(BF16)
    for r in range(rows):
        high, low = split_two(applied[r * p_size : (r + 1) * p_size, :])
        y = jnp.dot(place, high.astype(BF16), preferred_element_type=F32)
        y += jnp.dot(place, low.astype(BF16), preferred_element_type=F32)
        placed[pl.ds(r, n_blocks, stride=rows), :] = y

    for h in range(1, n_grp):
        across(h).wait_recv()
    factors = []
    for h in range(n_grp):
        who = lax.rem(g + h, n_grp)
        block = alpha[0, who] * mask[0, who].astype(F32)
        factors.append(
            [jnp.broadcast_to(block[:, s : s + 1], (rows, size)) for s in range(rows)]
        )

    def couple(t, _):
        at = pl.ds(pl.multiple_of(t * size, size), size)
        total = placed[pl.ds(pl.multiple_of(t * rows, rows), rows), :]
        for h in range(n_grp):
            if h == 0:
                c = coeff[:, at]
            else:
                c = partner[lax.rem(g + h, n_grp), :, at]
            for s in range(rows):
                total += factors[h][s] * jnp.broadcast_to(c[s : s + 1, :], (rows, size))
        out[:, at] = total
        return 0

    lax.fori_loop(0, n_blocks, couple, 0)

    def gather_up(d, _):
        back(d).wait_recv()
        who = lax.rem(w - d + n_wide, n_wide)
        out[:, columns(who)] += arrived[who]
        return 0

    out[:, columns(w)] += arrived[w]
    lax.fori_loop(1, n_wide, gather_up, 0)

    def drain(d, _):
        go(d).wait_send()
        back(d).wait_send()
        for h in range(1, n_grp):
            relay(d, h).wait_send()
        return 0

    for h in range(1, n_grp):
        relay(0, h).wait_send()
        across(h).wait_send()
    lax.fori_loop(1, n_wide, drain, 0)


def blocks_column(blocks, p_size):
    sublane = lax.broadcasted_iota(jnp.int32, (p_size, 1), 0)

    def put(k, column):
        return jnp.where(sublane == k, blocks[0, k], column)

    return lax.fori_loop(0, p_size, put, jnp.zeros((p_size, 1), jnp.int32))


def blocks_row(blocks, p_size):
    lane = lax.broadcasted_iota(jnp.int32, (1, p_size), 1)

    def put(k, row):
        return jnp.where(lane == k, blocks[1, k], row)

    return lax.fori_loop(0, p_size, put, jnp.zeros((1, p_size), jnp.int32))


def fused(n_grp, n_wide, args):
    coeff, beta, _, alpha, _, source, _, _, occupation, coulomb = args
    rows, width = coeff.shape
    cut = width // n_wide
    n_orb = occupation.shape[0]
    n_pair = coulomb.shape[0]
    n_strings = n_grp * n_wide * rows
    table_width = -(-n_pair // LANES) * LANES
    p_size, size = beta.shape[:2]
    vmem = pl.BlockSpec(memory_space=pltpu.VMEM)
    smem = pl.BlockSpec(memory_space=pltpu.SMEM)
    scratch = [
        pltpu.VMEM((n_grp * n_wide, rows, cut), F32),
        pltpu.VMEM((n_strings, cut), BF16),
        pltpu.VMEM((n_strings, cut), BF16),
        pltpu.VMEM((n_grp, rows, width), F32),
        pltpu.VMEM((n_wide, rows, cut), F32),
        pltpu.VMEM((n_wide, rows, cut), F32),
        pltpu.VMEM(beta.shape, F32),
        pltpu.VMEM((rows * p_size, size), F32),
        pltpu.VMEM((rows * p_size, size), F32),
        pltpu.VMEM((rows * p_size, size), F32),
        pltpu.VMEM((width // size * rows, size), F32),
        pltpu.VMEM((LANES, LANES), jnp.int32),
        pltpu.VMEM((LANES, LANES), jnp.int32),
        pltpu.VMEM((LANES, LANES), jnp.int32),
        pltpu.VMEM((LANES, LANES), F32),
        pltpu.VMEM((table_width, LANES), F32),
        pltpu.VMEM((LANES, table_width), F32),
        pltpu.VMEM((n_orb, rows, cut), F32),
        pltpu.VMEM((2 * n_orb * rows, rows * LANES), BF16),
        pltpu.VMEM((n_strings, rows * LANES), BF16),
        pltpu.VMEM((n_wide, n_orb * rows, n_strings), BF16),
        pltpu.VMEM((n_wide, n_orb * rows, n_strings), BF16),
        pltpu.SemaphoreType.DMA,
        pltpu.SemaphoreType.DMA((n_wide,)),
        pltpu.SemaphoreType.DMA((n_wide,)),
        pltpu.SemaphoreType.DMA((n_grp, n_wide)),
        pltpu.SemaphoreType.DMA((n_grp, n_wide)),
        pltpu.SemaphoreType.DMA((n_wide,)),
        pltpu.SemaphoreType.DMA((n_wide,)),
        pltpu.SemaphoreType.DMA((n_grp,)),
        pltpu.SemaphoreType.DMA((n_grp,)),
    ]
    return pl.pallas_call(
        functools.partial(kernel, n_grp, n_wide, n_orb),
        out_shape=jax.ShapeDtypeStruct(coeff.shape, F32),
        in_specs=[
            vmem,
            pl.BlockSpec(memory_space=pl.ANY),
            smem,
            vmem,
            smem,
            vmem,
            vmem,
            vmem,
            vmem,
            vmem,
        ],
        out_specs=vmem,
        scratch_shapes=scratch,
        compiler_params=pltpu.CompilerParams(
            collective_id=0, has_side_effects=True, vmem_limit_bytes=40 * 2**20
        ),
    )(*args)


def suits(n_grp, n_wide, args):
    coeff, beta, _, _, _, source, _, _, occupation, _ = args
    rows, width = coeff.shape
    n_orb = occupation.shape[0]
    return (
        n_grp > 1
        and n_wide > 1
        and rows == 8
        and width % (n_wide * LANES) == 0
        and beta.shape[1] == LANES
        and beta.shape[0] % 16 == 0
        and (width // LANES) % 16 == 0
        and n_orb % 2 == 0
        and source.shape[0] <= LANES
        and source.shape[1] == LANES
        and n_wide * rows == LANES
        and n_grp * n_wide * rows <= 512
    )


def general(
    coeff,
    beta_blocks,
    block_list,
    alpha_blocks,
    partner_mask,
    exc_source,
    exc_pair,
    exc_parity,
    occupation,
    coulomb,
):
    alpha_rows, beta_width = coeff.shape
    block_size = beta_blocks.shape[1]
    block_count = beta_width // block_size
    blocked = coeff.reshape(alpha_rows, block_count, block_size)
    block_ids = jnp.arange(block_count, dtype=jnp.int32)
    choosing = (block_list[0][:, None] == block_ids[None, :]).astype(jnp.float32)
    picked = jnp.einsum("rnk,pn->rpk", blocked, choosing, precision=HIGH)
    applied = jnp.einsum("rpk,pkl->rpl", picked, beta_blocks, precision=HIGH)
    placing = (block_list[1][:, None] == block_ids[None, :]).astype(jnp.float32)
    same_beta = jnp.einsum("rpl,pn->rnl", applied, placing, precision=HIGH).reshape(
        alpha_rows, beta_width
    )
    masked = alpha_blocks[0] * partner_mask[0][:, None, None].astype(jnp.float32)
    group_count = masked.shape[0]
    coupling = masked.transpose(1, 0, 2).reshape(alpha_rows, group_count * alpha_rows)
    same_alpha = jnp.dot(
        coupling,
        lax.all_gather(coeff, "grp", axis=0, tiled=True),
        precision=HIGH,
        preferred_element_type=jnp.float32,
    )
    beta_major = lax.all_to_all(coeff, "wide", split_axis=1, concat_axis=0, tiled=True)
    every_string = lax.all_gather(beta_major, "grp", axis=0, tiled=True)
    group_rows, slice_width = beta_major.shape
    replace_count = exc_source.shape[0]
    weights_local = jnp.dot(
        coulomb, occupation.astype(jnp.float32), precision=HIGH, preferred_element_type=jnp.float32
    )
    phases = 1.0 - 2.0 * exc_parity.astype(jnp.float32)
    row_block = 256 if group_rows % 256 == 0 else group_rows
    turns = group_rows // row_block

    def one_block(entry):
        sources, pairs, signs = entry
        fetched = jnp.take(every_string, sources, axis=0)
        factor = jnp.take(weights_local, pairs, axis=0)
        return jnp.sum(signs[:, :, None] * factor * fetched, axis=1)

    mixed_local = lax.map(
        one_block,
        (
            exc_source.T.reshape(turns, row_block, replace_count),
            exc_pair.T.reshape(turns, row_block, replace_count),
            phases.T.reshape(turns, row_block, replace_count),
        ),
    ).reshape(group_rows, slice_width)
    mixed = lax.all_to_all(mixed_local, "wide", split_axis=0, concat_axis=1, tiled=True)
    return same_beta + same_alpha + mixed


def per_device(n_grp, n_wide, *args):
    if suits(n_grp, n_wide, args):
        return fused(n_grp, n_wide, args)
    return general(*args)


def solution(mesh):
    in_specs = (
        P(("grp", "wide"), None),
        P(),
        P(),
        P(("grp", "wide"), None, None, None),
        P(("grp", "wide"), None),
        P(None, "grp"),
        P(None, "grp"),
        P(None, "grp"),
        P(None, "wide"),
        P(),
    )
    out_specs = P(("grp", "wide"), None)
    return jax.shard_map(
        functools.partial(per_device, mesh.shape["grp"], mesh.shape["wide"]),
        mesh=mesh, in_specs=in_specs,
        out_specs=out_specs,
        check_vma=False,
    )
```

```python
import functools

import jax
import jax.numpy as jnp
from jax import lax
from jax.experimental import pallas as pl
from jax.experimental.pallas import tpu as pltpu
from jax.sharding import PartitionSpec as P

HIGH = lax.Precision.HIGHEST
LANES = 128
MESH = pl.DeviceIdType.MESH
F32 = jnp.float32
BF16 = jnp.bfloat16


def split_two(x):
    high = x.astype(BF16).astype(F32)
    return high, x - high


def split_narrow(x):
    high = x.astype(BF16)
    return high, (x - high.astype(F32)).astype(BF16)


def kernel(
    n_grp,
    n_wide,
    coeff_hbm,
    beta_hbm,
    blocks_hbm,
    alpha_hbm,
    mask_hbm,
    source_hbm,
    pair_hbm,
    parity_hbm,
    occupation_hbm,
    coulomb_hbm,
    out,
    coeff,
    dense,
    blocks,
    alpha,
    mask,
    source,
    pair,
    parity,
    occupation,
    coulomb,
    strings,
    strings_three,
    partner,
    staged,
    arrived,
    picked_high,
    picked_low,
    applied,
    placed,
    padded,
    source_pad,
    pair_t,
    sign_t,
    table,
    occ,
    left,
    onehot,
    m_three,
    in_sem,
    go_send,
    go_recv,
    relay_send,
    relay_recv,
    mate_send,
    mate_recv,
    occ_send,
    occ_recv,
    back_send,
    back_recv,
    partner_send,
    partner_recv,
):
    g = lax.axis_index("grp")
    w = lax.axis_index("wide")
    chip = w // 2
    core = lax.rem(w, 2)
    n_chip = n_wide // 2
    mate = (g, 2 * chip + 1 - core)
    rows, width = coeff.shape
    cut = width // n_chip
    exc = source.shape[0]
    n_orb, n_pair = coulomb.shape
    chunks = table.shape[1] // LANES
    n_strings = n_grp * n_wide * rows
    n_m = n_orb * rows
    p_size, size = dense.shape[:2]
    n_blocks = width // size

    barrier = pltpu.get_barrier_semaphore()

    def greet(d, _):
        to = 2 * lax.rem(chip + d, n_chip) + core
        pl.semaphore_signal(barrier, inc=1, device_id=(g, to), device_id_type=MESH)
        return 0

    lax.fori_loop(1, n_chip, greet, 0)
    for h in range(1, n_grp):
        pl.semaphore_signal(
            barrier, inc=1, device_id=(lax.rem(g + h, n_grp), w), device_id_type=MESH
        )
    pl.semaphore_signal(barrier, inc=1, device_id=mate, device_id_type=MESH)

    fetches = [
        pltpu.make_async_copy(a, b, in_sem.at[i])
        for i, (a, b) in enumerate(
            (
                (pair_hbm, pair),
                (parity_hbm, parity),
                (source_hbm, source),
                (coulomb_hbm, coulomb),
                (occupation_hbm, occupation.at[core]),
                (coeff_hbm, coeff),
                (blocks_hbm, blocks),
                (alpha_hbm, alpha),
                (mask_hbm, mask),
                (beta_hbm, dense),
            )
        )
    ]
    for fetch in fetches:
        fetch.start()
    pl.semaphore_wait(barrier, n_chip - 1 + n_grp)

    def columns(j):
        return pl.ds(pl.multiple_of(j * cut, LANES), cut)

    def slot(d, h):
        group = lax.rem(g - h + n_grp, n_grp)
        return group * n_wide + 2 * lax.rem(chip - d + n_chip, n_chip) + core

    def go(d):
        to = lax.rem(chip + d, n_chip)
        return pltpu.make_async_remote_copy(
            src_ref=coeff_hbm.at[:, columns(to)],
            dst_ref=strings.at[g * n_wide + w],
            send_sem=go_send.at[d],
            recv_sem=go_recv.at[d],
            device_id=(g, 2 * to + core),
            device_id_type=MESH,
        )

    def relay(d, h):
        return pltpu.make_async_remote_copy(
            src_ref=strings.at[slot(d, 0)],
            dst_ref=strings.at[slot(d, 0)],
            send_sem=relay_send.at[h, d],
            recv_sem=relay_recv.at[h, d],
            device_id=(lax.rem(g + h, n_grp), w),
            device_id_type=MESH,
        )

    def to_mate(d, h):
        return pltpu.make_async_remote_copy(
            src_ref=strings.at[slot(d, h)],
            dst_ref=strings.at[slot(d, h)],
            send_sem=mate_send.at[h, d],
            recv_sem=mate_recv.at[h, d],
            device_id=mate,
            device_id_type=MESH,
        )

    occ_copy = pltpu.make_async_remote_copy(
        src_ref=occupation_hbm,
        dst_ref=occupation.at[core],
        send_sem=occ_send,
        recv_sem=occ_recv,
        device_id=mate,
        device_id_type=MESH,
    )

    def back(d):
        to = lax.rem(chip + d, n_chip)
        return pltpu.make_async_remote_copy(
            src_ref=staged.at[to],
            dst_ref=arrived.at[chip],
            send_sem=back_send.at[d],
            recv_sem=back_recv.at[d],
            device_id=(g, 2 * to + core),
            device_id_type=MESH,
        )

    def across(h):
        return pltpu.make_async_remote_copy(
            src_ref=coeff_hbm,
            dst_ref=partner.at[g],
            send_sem=partner_send.at[h],
            recv_sem=partner_recv.at[h],
            device_id=(lax.rem(g + h, n_grp), w),
            device_id_type=MESH,
        )

    def start_go(d, _):
        go(d).start()
        return 0

    lax.fori_loop(1, n_chip, start_go, 0)
    occ_copy.start()

    padded[...] = jnp.zeros_like(padded)
    onehot[...] = jnp.zeros_like(onehot)
    table[...] = jnp.zeros_like(table)
    fetches[0].wait()
    padded[0:exc, :] = pair[...]
    pair_t[...] = padded[...].T
    fetches[1].wait()
    padded[0:exc, :] = 1 - 2 * parity[...]
    sign_t[...] = padded[...].T.astype(F32)
    source_pad[...] = jnp.zeros_like(source_pad)
    fetches[2].wait()
    source_pad[0:exc, :] = source[...]
    fetches[3].wait()
    table[0:n_orb, 0:n_pair] = coulomb[...]
    fetches[5].wait()
    strings[g * n_wide + w] = coeff[:, columns(chip)]
    partner[g] = coeff[...]
    for h in range(1, n_grp):
        relay(0, h).start()
    to_mate(0, 0).start()

    def build(to):
        block = 2 * to + core
        at = pl.ds(pl.multiple_of(block * rows, rows), rows)
        pairs = pair_t[at, :]
        signs = sign_t[at, :]
        which = pairs // LANES
        lane = pairs - which * LANES
        sublane = lax.broadcasted_iota(jnp.int32, (rows, LANES), 0)
        string = lax.broadcasted_iota(jnp.int32, (16, n_strings), 1)
        for a in range(rows):
            column = jnp.full((rows, LANES), block * rows + a, jnp.int32)
            for e in range(0, exc, 16):
                pieces = [
                    jnp.take_along_axis(
                        source_pad[e + f : e + f + rows, :],
                        column,
                        axis=1,
                        mode="promise_in_bounds",
                    )
                    for f in (0, 8)
                ]
                both = jnp.concatenate(pieces, axis=0)
                full = jnp.concatenate([both] * (n_strings // LANES), axis=1)
                onehot[a * LANES + e : a * LANES + e + 16, :] = jnp.where(
                    full == string, 1.0, 0.0
                ).astype(BF16)
        for r in range(0, n_orb, 2):
            halves = []
            for q in (r, r + 1):
                value = None
                for c in range(chunks):
                    line = jnp.broadcast_to(
                        table[q : q + 1, c * LANES : (c + 1) * LANES], (rows, LANES)
                    )
                    got = jnp.take_along_axis(line, lane, axis=1, mode="promise_in_bounds")
                    value = got if value is None else jnp.where(which == c, got, value)
                halves.append(split_two(value * signs))
            for part in range(2):
                base = part * n_m + r * rows
                for a in range(rows):
                    both = jnp.concatenate(
                        [jnp.where(sublane == a, half[part], 0.0) for half in halves], axis=0
                    )
                    left[base : base + 2 * rows, a * LANES : (a + 1) * LANES] = both.astype(BF16)
        m = jnp.dot(left[...], onehot[...], preferred_element_type=F32)
        high, low = split_narrow(m[:n_m] + m[n_m:])
        m_three[to, :, 0:n_strings] = high
        m_three[to, :, n_strings : 2 * n_strings] = low
        m_three[to, :, 2 * n_strings :] = high

    build(0)

    def build_and_pass(d, _):
        build(d)
        go(d).wait_recv()
        for h in range(1, n_grp):
            relay(d, h).start()
        to_mate(d, 0).start()
        return 0

    lax.fori_loop(1, n_chip, build_and_pass, 0)
    for h in range(1, n_grp):
        across(h).start()

    fetches[6].wait()
    padded[0:2, 0:p_size] = blocks[...]
    blocks_t = padded[...].T
    for t in range(n_blocks):
        placed[t * rows : (t + 1) * rows, :] = coeff[:, t * size : (t + 1) * size]
    choose = jnp.where(
        lax.broadcasted_iota(jnp.int32, (p_size, n_blocks), 1)
        == jnp.broadcast_to(blocks_t[0:p_size, 0:1], (p_size, n_blocks)),
        1.0,
        0.0,
    ).astype(BF16)
    for r in range(rows):
        high, low = split_narrow(placed[pl.ds(r, n_blocks, stride=rows), :])
        both = jnp.dot(
            choose, jnp.concatenate([high, low], axis=1), preferred_element_type=F32
        )
        picked_high[pl.ds(r, p_size, stride=rows), :] = both[:, :size]
        picked_low[pl.ds(r, p_size, stride=rows), :] = both[:, size:]
    fetches[9].wait()

    def pick(k):
        at = pl.ds(pl.multiple_of(k * rows, rows), rows)
        high, low = picked_high[at, :], picked_low[at, :]
        return [
            jnp.concatenate([high, high], axis=1),
            jnp.concatenate([low, jnp.zeros_like(low)], axis=1),
        ]

    share = p_size // n_chip

    def dense_and_pass(d, _):
        results = []
        for i in range(0, share, 2):
            k = d * share + i
            lhs = jnp.concatenate(pick(k) + pick(k + 1), axis=0).astype(BF16)
            h0, l0 = split_narrow(dense[k])
            h1, l1 = split_narrow(dense[k + 1])
            rhs = jnp.concatenate(
                [jnp.concatenate([h0, h1], axis=1), jnp.concatenate([l0, l1], axis=1)], axis=0
            )
            y = jnp.dot(lhs, rhs, preferred_element_type=F32)
            results.append(y[0:rows, :size] + y[rows : 2 * rows, :size])
            results.append(y[2 * rows : 3 * rows, size:] + y[3 * rows :, size:])
        for i, result in enumerate(results):
            applied[pl.ds(d * share + i, rows, stride=p_size), :] = result
        for h in range(1, n_grp):
            relay(d, h).wait_recv()
            to_mate(d, h).start()
        return 0

    lax.fori_loop(0, n_chip, dense_and_pass, 0)

    fetches[4].wait()
    occ_copy.wait_recv()
    half = occupation.shape[2]
    for r in range(n_orb):
        for q in range(2):
            occ[r, :, q * half : (q + 1) * half] = jnp.broadcast_to(
                occupation[q, r : r + 1, :].astype(F32), (rows, half)
            )

    def wait_mate(d, _):
        for h in range(n_grp):
            to_mate(d, h).wait_recv()
        return 0

    lax.fori_loop(0, n_chip, wait_mate, 0)
    high, low = split_narrow(strings[...].reshape(n_strings, cut))
    strings_three[0:n_strings, :] = high
    strings_three[n_strings : 2 * n_strings, :] = high
    strings_three[2 * n_strings :, :] = low

    def mix_two(i, _):
        d = 2 * i + 1
        tos = [lax.rem(chip + d, n_chip), lax.rem(chip + d + 1, n_chip)]
        y = jnp.dot(
            jnp.concatenate([m_three[to] for to in tos], axis=0),
            strings_three[...],
            preferred_element_type=F32,
        )
        for q in range(2):
            total = y[q * n_m : q * n_m + rows] * occ[0]
            for r in range(1, n_orb):
                total += y[q * n_m + r * rows : q * n_m + (r + 1) * rows] * occ[r]
            staged[tos[q]] = total
        back(d).start()

        @pl.when(d + 1 < n_chip)
        def _():
            back(d + 1).start()

        return 0

    lax.fori_loop(0, n_chip // 2, mix_two, 0)

    place = jnp.where(
        lax.broadcasted_iota(jnp.int32, (n_blocks, p_size), 0)
        == jnp.broadcast_to(blocks[1:2, :], (n_blocks, p_size)),
        1.0,
        0.0,
    ).astype(BF16)
    place = jnp.concatenate([place, place], axis=1)
    for r in range(0, rows, 2):
        parts = [split_narrow(applied[q * p_size : (q + 1) * p_size, :]) for q in (r, r + 1)]
        both = jnp.concatenate(
            [jnp.concatenate([part[i] for part in parts], axis=1) for i in range(2)], axis=0
        )
        y = jnp.dot(place, both, preferred_element_type=F32)
        placed[pl.ds(r, n_blocks, stride=rows), :] = y[:, :size]
        placed[pl.ds(r + 1, n_blocks, stride=rows), :] = y[:, size:]

    fetches[7].wait()
    fetches[8].wait()
    factors = []
    for h in range(n_grp):
        block = alpha[0, h] * mask[0:1, h : h + 1].astype(F32)
        factors.append(
            [jnp.broadcast_to(block[:, s : s + 1], (rows, size)) for s in range(rows)]
        )
    for h in range(1, n_grp):
        across(h).wait_recv()

    def couple(i, _):
        for j in range(4):
            t = 4 * i + j
            at = pl.ds(pl.multiple_of(t * size, size), size)
            total = placed[pl.ds(pl.multiple_of(t * rows, rows), rows), :]
            for h in range(n_grp):
                c = partner[h, :, at]
                for s in range(rows):
                    total += factors[h][s] * jnp.broadcast_to(c[s : s + 1, :], (rows, size))
            out[:, at] = total
        return 0

    lax.fori_loop(0, n_blocks // 4, couple, 0)

    out[:, columns(chip)] += staged[chip]

    def gather_up(d, _):
        back(d).wait_recv()
        who = lax.rem(chip - d + n_chip, n_chip)
        out[:, columns(who)] += arrived[who]
        return 0

    lax.fori_loop(1, n_chip, gather_up, 0)

    def drain(d, _):
        go(d).wait_send()
        back(d).wait_send()
        return 0

    lax.fori_loop(1, n_chip, drain, 0)

    def drain_passed(d, _):
        to_mate(d, 0).wait_send()
        for h in range(1, n_grp):
            relay(d, h).wait_send()
            to_mate(d, h).wait_send()
        return 0

    lax.fori_loop(0, n_chip, drain_passed, 0)
    occ_copy.wait_send()
    for h in range(1, n_grp):
        across(h).wait_send()


def fused(n_grp, n_wide, args):
    coeff, beta, blocks, alpha, mask, source, pair, parity, occupation, coulomb = args
    coulomb = coulomb.T
    rows, width = coeff.shape
    n_chip = n_wide // 2
    cut = width // n_chip
    n_orb, n_pair = coulomb.shape
    n_m = n_orb * rows
    n_strings = n_grp * n_wide * rows
    table_width = -(-n_pair // LANES) * LANES
    p_size, size = beta.shape[:2]
    operands = (coeff, beta, blocks, alpha, mask, source, pair, parity, occupation, coulomb)
    landing = [pltpu.VMEM(x.shape, x.dtype) for x in operands]
    landing[8] = pltpu.VMEM((2,) + occupation.shape, occupation.dtype)
    dma = pltpu.SemaphoreType.DMA
    scratch = landing + [
        pltpu.VMEM((n_grp * n_wide, rows, cut), F32),
        pltpu.VMEM((3 * n_strings, cut), BF16),
        pltpu.VMEM((n_grp, rows, width), F32),
        pltpu.VMEM((n_chip, rows, cut), F32),
        pltpu.VMEM((n_chip, rows, cut), F32),
        pltpu.VMEM((rows * p_size, size), F32),
        pltpu.VMEM((rows * p_size, size), F32),
        pltpu.VMEM((rows * p_size, size), F32),
        pltpu.VMEM((width // size * rows, size), F32),
        pltpu.VMEM((LANES, LANES), jnp.int32),
        pltpu.VMEM((LANES, LANES), jnp.int32),
        pltpu.VMEM((LANES, LANES), jnp.int32),
        pltpu.VMEM((LANES, LANES), F32),
        pltpu.VMEM((-(-n_orb // 8) * 8, table_width), F32),
        pltpu.VMEM((n_orb, rows, cut), F32),
        pltpu.VMEM((2 * n_m, rows * LANES), BF16),
        pltpu.VMEM((rows * LANES, n_strings), BF16),
        pltpu.VMEM((n_chip, n_m, 3 * n_strings), BF16),
        dma((len(operands),)),
        dma((n_chip,)),
        dma((n_chip,)),
        dma((n_grp, n_chip)),
        dma((n_grp, n_chip)),
        dma((n_grp, n_chip)),
        dma((n_grp, n_chip)),
        dma,
        dma,
        dma((n_chip,)),
        dma((n_chip,)),
        dma((n_grp,)),
        dma((n_grp,)),
    ]
    return pl.pallas_call(
        functools.partial(kernel, n_grp, n_wide),
        out_shape=jax.ShapeDtypeStruct(coeff.shape, F32),
        in_specs=[pl.BlockSpec(memory_space=pltpu.HBM)] * len(operands),
        out_specs=pl.BlockSpec(memory_space=pltpu.VMEM),
        scratch_shapes=scratch,
        compiler_params=pltpu.CompilerParams(
            collective_id=0, has_side_effects=True, vmem_limit_bytes=64 * 2**20 - 2**16
        ),
    )(*operands)


def suits(n_grp, n_wide, args):
    coeff, beta, _, _, _, source, _, _, occupation, _ = args
    rows, width = coeff.shape
    n_orb = occupation.shape[0]
    n_strings = n_grp * n_wide * rows
    return (
        n_grp > 1
        and n_wide > 2
        and n_wide % 4 == 0
        and rows == 8
        and width % (n_wide * LANES) == 0
        and beta.shape[1] == LANES
        and beta.shape[0] % (2 * n_wide // 2) == 0
        and beta.shape[0] <= LANES
        and width // LANES % 16 == 0
        and n_orb % 2 == 0
        and source.shape[0] <= LANES
        and source.shape[1] == LANES
        and n_wide * rows == LANES
        and n_strings % LANES == 0
        and n_strings <= 512
    )


def general(
    coeff,
    beta_blocks,
    block_list,
    alpha_blocks,
    partner_mask,
    exc_source,
    exc_pair,
    exc_parity,
    occupation,
    coulomb,
):
    alpha_rows, beta_width = coeff.shape
    block_size = beta_blocks.shape[1]
    block_count = beta_width // block_size
    blocked = coeff.reshape(alpha_rows, block_count, block_size)
    block_ids = jnp.arange(block_count, dtype=jnp.int32)
    choosing = (block_list[0][:, None] == block_ids[None, :]).astype(jnp.float32)
    picked = jnp.einsum("rnk,pn->rpk", blocked, choosing, precision=HIGH)
    applied = jnp.einsum("rpk,pkl->rpl", picked, beta_blocks, precision=HIGH)
    placing = (block_list[1][:, None] == block_ids[None, :]).astype(jnp.float32)
    same_beta = jnp.einsum("rpl,pn->rnl", applied, placing, precision=HIGH).reshape(
        alpha_rows, beta_width
    )
    masked = alpha_blocks[0] * partner_mask[0][:, None, None].astype(jnp.float32)
    group_count = masked.shape[0]
    coupling = masked.transpose(1, 0, 2).reshape(alpha_rows, group_count * alpha_rows)
    same_alpha = jnp.dot(
        coupling,
        lax.all_gather(coeff, "grp", axis=0, tiled=True),
        precision=HIGH,
        preferred_element_type=jnp.float32,
    )
    beta_major = lax.all_to_all(coeff, "wide", split_axis=1, concat_axis=0, tiled=True)
    every_string = lax.all_gather(beta_major, "grp", axis=0, tiled=True)
    group_rows, slice_width = beta_major.shape
    replace_count = exc_source.shape[0]
    weights_local = jnp.dot(
        coulomb, occupation.astype(jnp.float32), precision=HIGH, preferred_element_type=jnp.float32
    )
    phases = 1.0 - 2.0 * exc_parity.astype(jnp.float32)
    row_block = 256 if group_rows % 256 == 0 else group_rows
    turns = group_rows // row_block

    def one_block(entry):
        sources, pairs, signs = entry
        fetched = jnp.take(every_string, sources, axis=0)
        factor = jnp.take(weights_local, pairs, axis=0)
        return jnp.sum(signs[:, :, None] * factor * fetched, axis=1)

    mixed_local = lax.map(
        one_block,
        (
            exc_source.T.reshape(turns, row_block, replace_count),
            exc_pair.T.reshape(turns, row_block, replace_count),
            phases.T.reshape(turns, row_block, replace_count),
        ),
    ).reshape(group_rows, slice_width)
    mixed = lax.all_to_all(mixed_local, "wide", split_axis=0, concat_axis=1, tiled=True)
    return same_beta + same_alpha + mixed


def per_device(n_grp, n_wide, *args):
    if suits(n_grp, n_wide, args):
        return fused(n_grp, n_wide, args)
    return general(*args)


def solution(mesh):
    in_specs = (
        P(("grp", "wide"), None),
        P(),
        P(),
        P(("grp", "wide"), None, None, None),
        P(("grp", "wide"), None),
        P(None, "grp"),
        P(None, "grp"),
        P(None, "grp"),
        P(None, "wide"),
        P(),
    )
    out_specs = P(("grp", "wide"), None)
    return jax.shard_map(
        functools.partial(per_device, mesh.shape["grp"], mesh.shape["wide"]),
        mesh=mesh, in_specs=in_specs,
        out_specs=out_specs,
        check_vma=False,
    )
```

```python
import functools

import jax
import jax.numpy as jnp
from jax import lax
from jax.experimental import pallas as pl
from jax.experimental.pallas import tpu as pltpu
from jax.sharding import PartitionSpec as P

HIGH = lax.Precision.HIGHEST
LANES = 128
MESH = pl.DeviceIdType.MESH
F32 = jnp.float32
BF16 = jnp.bfloat16


def split_two(x):
    high = x.astype(BF16).astype(F32)
    return high, x - high


def split_narrow(x):
    high = x.astype(BF16)
    return high, (x - high.astype(F32)).astype(BF16)


def kernel(
    n_grp,
    n_wide,
    coeff_hbm,
    beta_hbm,
    blocks_hbm,
    alpha_hbm,
    mask_hbm,
    source_hbm,
    pair_hbm,
    parity_hbm,
    occupation_hbm,
    coulomb_hbm,
    same,
    mixed,
    coeff,
    dense,
    blocks,
    alpha,
    mask,
    source,
    pair,
    parity,
    occupation,
    coulomb,
    strings,
    strings_three,
    partner,
    staged,
    same_vmem,
    tiles,
    blocks_smem,
    applied,
    placed,
    padded,
    source_pad,
    pair_t,
    sign_t,
    coulomb_pad,
    table,
    occ,
    m_three,
    in_sem,
    out_sem,
    go_send,
    go_recv,
    relay_send,
    relay_recv,
    mate_send,
    mate_recv,
    occ_send,
    occ_recv,
    back_send,
    back_recv,
    partner_send,
    partner_recv,
):
    g = lax.axis_index("grp")
    w = lax.axis_index("wide")
    chip = w // 2
    core = lax.rem(w, 2)
    n_chip = n_wide // 2
    mate = (g, 2 * chip + 1 - core)
    rows, width = coeff.shape
    cut = width // n_chip
    exc = source.shape[0]
    n_orb, n_pair = coulomb.shape
    chunks = table.shape[0]
    n_strings = n_grp * n_wide * rows
    n_r = -(-n_orb // 4) * 8
    n_m = rows // 2 * n_r
    p_size, size = dense.shape[:2]
    n_blocks = width // size

    barrier = pltpu.get_barrier_semaphore()

    def greet(d, _):
        to = 2 * lax.rem(chip + d, n_chip) + core
        pl.semaphore_signal(barrier, inc=1, device_id=(g, to), device_id_type=MESH)
        return 0

    lax.fori_loop(1, n_chip, greet, 0)
    for h in range(1, n_grp):
        pl.semaphore_signal(
            barrier, inc=1, device_id=(lax.rem(g + h, n_grp), w), device_id_type=MESH
        )
    pl.semaphore_signal(barrier, inc=1, device_id=mate, device_id_type=MESH)

    fetches = [
        pltpu.make_async_copy(a, b, in_sem.at[i])
        for i, (a, b) in enumerate(
            (
                (pair_hbm, pair),
                (parity_hbm, parity),
                (source_hbm, source),
                (coulomb_hbm, coulomb),
                (occupation_hbm, occupation.at[core]),
                (coeff_hbm, coeff),
                (blocks_hbm, blocks),
                (alpha_hbm, alpha),
                (mask_hbm, mask),
                (beta_hbm, dense),
                (blocks_hbm, blocks_smem),
            )
        )
    ]
    for fetch in fetches:
        fetch.start()
    pl.semaphore_wait(barrier, n_chip - 1 + n_grp)

    def columns(j):
        return pl.ds(pl.multiple_of(j * cut, LANES), cut)

    def slot(d, h):
        group = lax.rem(g - h + n_grp, n_grp)
        return group * n_wide + 2 * lax.rem(chip - d + n_chip, n_chip) + core

    def go(d):
        to = lax.rem(chip + d, n_chip)
        return pltpu.make_async_remote_copy(
            src_ref=coeff_hbm.at[:, columns(to)],
            dst_ref=strings.at[g * n_wide + w],
            send_sem=go_send.at[d],
            recv_sem=go_recv.at[d],
            device_id=(g, 2 * to + core),
            device_id_type=MESH,
        )

    def relay(d, h):
        return pltpu.make_async_remote_copy(
            src_ref=strings.at[slot(d, 0)],
            dst_ref=strings.at[slot(d, 0)],
            send_sem=relay_send.at[h, d],
            recv_sem=relay_recv.at[h, d],
            device_id=(lax.rem(g + h, n_grp), w),
            device_id_type=MESH,
        )

    def to_mate(d, h):
        return pltpu.make_async_remote_copy(
            src_ref=strings.at[slot(d, h)],
            dst_ref=strings.at[slot(d, h)],
            send_sem=mate_send.at[h, d],
            recv_sem=mate_recv.at[h, d],
            device_id=mate,
            device_id_type=MESH,
        )

    occ_copy = pltpu.make_async_remote_copy(
        src_ref=occupation_hbm,
        dst_ref=occupation.at[core],
        send_sem=occ_send,
        recv_sem=occ_recv,
        device_id=mate,
        device_id_type=MESH,
    )

    def back(d):
        to = lax.rem(chip + d, n_chip)
        return pltpu.make_async_remote_copy(
            src_ref=staged.at[to],
            dst_ref=mixed.at[:, columns(chip)],
            send_sem=back_send.at[d],
            recv_sem=back_recv.at[d],
            device_id=(g, 2 * to + core),
            device_id_type=MESH,
        )

    def across(h):
        return pltpu.make_async_remote_copy(
            src_ref=coeff_hbm,
            dst_ref=partner.at[g],
            send_sem=partner_send.at[h],
            recv_sem=partner_recv.at[h],
            device_id=(lax.rem(g + h, n_grp), w),
            device_id_type=MESH,
        )

    def start_go(d, _):
        go(d).start()
        return 0

    lax.fori_loop(1, n_chip, start_go, 0)
    occ_copy.start()

    padded[...] = jnp.zeros_like(padded)
    occ[...] = jnp.zeros_like(occ)
    table[...] = jnp.zeros_like(table)
    fetches[0].wait()
    padded[0:exc, :] = pair[...]
    pair_t[...] = padded[...].T
    fetches[1].wait()
    padded[0:exc, :] = 1 - 2 * parity[...]
    sign_t[...] = padded[...].T.astype(F32)
    source_pad[...] = jnp.zeros_like(source_pad)
    fetches[2].wait()
    source_pad[0:exc, :] = source[...]
    fetches[3].wait()
    coulomb_pad[...] = jnp.zeros_like(coulomb_pad)
    coulomb_pad[:, 0:n_pair] = coulomb[...]
    for q in range(2):
        for c in range(chunks):
            line = coulomb_pad[:, c * LANES : (c + 1) * LANES]
            table[c, pl.ds(q, n_orb, stride=2), :] = line
    fetches[5].wait()
    strings[g * n_wide + w] = coeff[:, columns(chip)]
    partner[g] = coeff[...]
    for h in range(1, n_grp):
        relay(0, h).start()
    to_mate(0, 0).start()

    def build(to):
        block = 2 * to + core
        at = pl.ds(pl.multiple_of(block * rows, rows), rows)
        sublane = lax.broadcasted_iota(jnp.int32, (rows, LANES), 0)
        odd = sublane - sublane // 2 * 2 == 1
        string = lax.broadcasted_iota(jnp.int32, (16, n_strings), 1)
        all_pairs = pair_t[at, :]
        all_signs = sign_t[at, :]

        def of_two(x, a):
            return jnp.where(
                odd,
                jnp.broadcast_to(x[a + 1 : a + 2, :], (rows, LANES)),
                jnp.broadcast_to(x[a : a + 1, :], (rows, LANES)),
            )

        found = []
        for a in range(0, rows, 2):
            hits = []
            for b in (a, a + 1):
                column = jnp.full((rows, LANES), block * rows + b, jnp.int32)
                for e in range(0, LANES, 16):
                    if e >= exc:
                        hits.append(jnp.zeros((16, n_strings), BF16))
                        continue
                    pieces = [
                        jnp.take_along_axis(
                            source_pad[e + f : e + f + rows, :],
                            column,
                            axis=1,
                            mode="promise_in_bounds",
                        )
                        for f in (0, 8)
                    ]
                    both = jnp.concatenate(pieces, axis=0)
                    full = jnp.concatenate([both] * (n_strings // LANES), axis=1)
                    hits.append(jnp.where(full == string, 1.0, 0.0).astype(BF16))
            pairs = of_two(all_pairs, a)
            signs = of_two(all_signs, a)
            which = pairs // LANES
            lane = pairs - which * LANES
            parts = [[], []]
            for r in range(0, n_r, rows):
                value = None
                for c in range(chunks):
                    got = jnp.take_along_axis(
                        table[c, r : r + rows, :],
                        lane,
                        axis=1,
                        mode="promise_in_bounds",
                    )
                    value = got if value is None else jnp.where(which == c, got, value)
                for part, half in zip(parts, split_two(value * signs)):
                    part.append(
                        jnp.concatenate(
                            [jnp.where(odd, 0.0, half), jnp.where(odd, half, 0.0)], axis=1
                        )
                    )
            left = jnp.concatenate(parts[0] + parts[1], axis=0).astype(BF16)
            m = jnp.dot(left, jnp.concatenate(hits, axis=0), preferred_element_type=F32)
            found.append(m[:n_r] + m[n_r:])
        return split_narrow(jnp.concatenate(found, axis=0))

    def build_and_pass(i, _):
        d = 2 * i
        for to, (high, low) in [(q, build(q)) for q in (d, d + 1)]:
            m_three[to, :, 0:n_strings] = high
            m_three[to, :, n_strings : 2 * n_strings] = low
            m_three[to, :, 2 * n_strings :] = high

        @pl.when(i > 0)
        def _():
            pass_on(d)

        pass_on(d + 1)
        return 0

    def pass_on(d):
        go(d).wait_recv()
        for h in range(1, n_grp):
            relay(d, h).start()
        to_mate(d, 0).start()

    lax.fori_loop(0, n_chip // 2, build_and_pass, 0)
    for h in range(1, n_grp):
        across(h).start()

    fetches[10].wait()
    for t in range(n_blocks):
        tiles[t] = coeff[:, t * size : (t + 1) * size]
    fetches[9].wait()

    def pick(k):
        high, low = split_two(tiles[blocks_smem[0, k]])
        return [
            jnp.concatenate([high, high], axis=1),
            jnp.concatenate([low, jnp.zeros_like(low)], axis=1),
        ]

    share = p_size // n_chip

    def dense_and_pass(d, _):
        results = []
        for i in range(0, share, 2):
            k = d * share + i
            lhs = jnp.concatenate(pick(k) + pick(k + 1), axis=0).astype(BF16)
            h0, l0 = split_narrow(dense[k])
            h1, l1 = split_narrow(dense[k + 1])
            rhs = jnp.concatenate(
                [jnp.concatenate([h0, h1], axis=1), jnp.concatenate([l0, l1], axis=1)], axis=0
            )
            y = jnp.dot(lhs, rhs, preferred_element_type=F32)
            results.append(y[0:rows, :size] + y[rows : 2 * rows, :size])
            results.append(y[2 * rows : 3 * rows, size:] + y[3 * rows :, size:])
        for i, result in enumerate(results):
            applied[pl.ds(d * share + i, rows, stride=p_size), :] = result
        for h in range(1, n_grp):
            relay(d, h).wait_recv()
            to_mate(d, h).start()
        return 0

    lax.fori_loop(0, n_chip, dense_and_pass, 0)

    fetches[4].wait()
    occ_copy.wait_recv()
    half = occupation.shape[2]
    for q in range(2):
        for r in range(2):
            for c in range(0, half, LANES):
                occ[(q * half + c) // LANES, pl.ds(r, n_orb, stride=2), :] = (
                    occupation[q, :, c : c + LANES].astype(F32)
                )

    def wait_mate(d, _):
        for h in range(n_grp):
            to_mate(d, h).wait_recv()
        return 0

    lax.fori_loop(0, n_chip, wait_mate, 0)
    high, low = split_narrow(strings[...].reshape(n_strings, cut))
    strings_three[0:n_strings, :] = high
    strings_three[n_strings : 2 * n_strings, :] = high
    strings_three[2 * n_strings :, :] = low

    def reduce_rows(y):
        sublane = lax.broadcasted_iota(jnp.int32, (rows, cut), 0)
        factor = [
            jnp.concatenate([occ[c, r : r + rows, :] for c in range(cut // LANES)], axis=1)
            for r in range(0, n_r, rows)
        ]
        total = None
        for p in range(rows // 2):
            z = y[p * n_r : p * n_r + rows] * factor[0]
            for r in range(rows, n_r, rows):
                z += y[p * n_r + r : p * n_r + r + rows] * factor[r // rows]
            z += pltpu.roll(z, 4, 0)
            z += pltpu.roll(z, 2, 0)
            total = z if total is None else jnp.where(sublane // 2 == p, z, total)
        return total

    def mix_four(i, _):
        d = 4 * i + 1
        tos = [lax.rem(chip + d + q, n_chip) for q in range(4)]
        for q in (0, 2):
            y = jnp.dot(
                jnp.concatenate([m_three[to] for to in tos[q : q + 2]], axis=0),
                strings_three[...],
                preferred_element_type=F32,
            )
            staged[tos[q]] = reduce_rows(y[:n_m])
            staged[tos[q + 1]] = reduce_rows(y[n_m:])
        for q in range(3):
            back(d + q).start()

        @pl.when(d + 3 < n_chip)
        def _():
            back(d + 3).start()

        return 0

    lax.fori_loop(0, n_chip // 4, mix_four, 0)
    own = pltpu.make_async_copy(staged.at[chip], mixed.at[:, columns(chip)], out_sem.at[0])
    own.start()

    fetches[6].wait()
    place = jnp.where(
        lax.broadcasted_iota(jnp.int32, (n_blocks, p_size), 0)
        == jnp.broadcast_to(blocks[1:2, :], (n_blocks, p_size)),
        1.0,
        0.0,
    ).astype(BF16)
    place = jnp.concatenate([place, place], axis=1)
    for r in range(0, rows, 2):
        parts = [split_narrow(applied[q * p_size : (q + 1) * p_size, :]) for q in (r, r + 1)]
        both = jnp.concatenate(
            [jnp.concatenate([part[i] for part in parts], axis=1) for i in range(2)], axis=0
        )
        y = jnp.dot(place, both, preferred_element_type=F32)
        placed[pl.ds(r, n_blocks, stride=rows), :] = y[:, :size]
        placed[pl.ds(r + 1, n_blocks, stride=rows), :] = y[:, size:]

    fetches[7].wait()
    fetches[8].wait()
    factors = []
    for h in range(n_grp):
        block = alpha[0, h] * mask[0:1, h : h + 1].astype(F32)
        factors.append(
            [jnp.broadcast_to(block[:, s : s + 1], (rows, size)) for s in range(rows)]
        )
    for h in range(1, n_grp):
        across(h).wait_recv()

    def couple(i, _):
        for j in range(4):
            t = 4 * i + j
            at = pl.ds(pl.multiple_of(t * size, size), size)
            total = placed[pl.ds(pl.multiple_of(t * rows, rows), rows), :]
            for h in range(n_grp):
                c = partner[h, :, at]
                for s in range(rows):
                    total += factors[h][s] * jnp.broadcast_to(c[s : s + 1, :], (rows, size))
            same_vmem[:, at] = total
        return 0

    lax.fori_loop(0, n_blocks // 4, couple, 0)

    write = pltpu.make_async_copy(same_vmem, same, out_sem.at[1])
    write.start()

    def drain(d, _):
        go(d).wait_send()
        back(d).wait()
        return 0

    lax.fori_loop(1, n_chip, drain, 0)

    def drain_passed(d, _):
        to_mate(d, 0).wait_send()
        for h in range(1, n_grp):
            relay(d, h).wait_send()
            to_mate(d, h).wait_send()
        return 0

    lax.fori_loop(0, n_chip, drain_passed, 0)
    occ_copy.wait_send()
    for h in range(1, n_grp):
        across(h).wait_send()
    own.wait()
    write.wait()


def fused(n_grp, n_wide, args):
    coeff, beta, blocks, alpha, mask, source, pair, parity, occupation, coulomb = args
    coulomb = coulomb.T
    rows, width = coeff.shape
    n_chip = n_wide // 2
    cut = width // n_chip
    n_orb, n_pair = coulomb.shape
    n_r = -(-n_orb // 4) * 8
    n_m = rows // 2 * n_r
    n_strings = n_grp * n_wide * rows
    table_width = -(-n_pair // LANES) * LANES
    p_size, size = beta.shape[:2]
    operands = (coeff, beta, blocks, alpha, mask, source, pair, parity, occupation, coulomb)
    landing = [pltpu.VMEM(x.shape, x.dtype) for x in operands]
    landing[8] = pltpu.VMEM((2,) + occupation.shape, occupation.dtype)
    dma = pltpu.SemaphoreType.DMA
    scratch = landing + [
        pltpu.VMEM((n_grp * n_wide, rows, cut), F32),
        pltpu.VMEM((3 * n_strings, cut), BF16),
        pltpu.VMEM((n_grp, rows, width), F32),
        pltpu.VMEM((n_chip, rows, cut), F32),
        pltpu.VMEM((rows, width), F32),
        pltpu.VMEM((width // size, rows, size), F32),
        pltpu.SMEM(blocks.shape, blocks.dtype),
        pltpu.VMEM((rows * p_size, size), F32),
        pltpu.VMEM((width // size * rows, size), F32),
        pltpu.VMEM((LANES, LANES), jnp.int32),
        pltpu.VMEM((LANES, LANES), jnp.int32),
        pltpu.VMEM((LANES, LANES), jnp.int32),
        pltpu.VMEM((LANES, LANES), F32),
        pltpu.VMEM((n_orb, table_width), F32),
        pltpu.VMEM((table_width // LANES, n_r, LANES), F32),
        pltpu.VMEM((cut // LANES, n_r, LANES), F32),
        pltpu.VMEM((n_chip, n_m, 3 * n_strings), BF16),
        dma((len(operands) + 1,)),
        dma((2,)),
        dma((n_chip,)),
        dma((n_chip,)),
        dma((n_grp, n_chip)),
        dma((n_grp, n_chip)),
        dma((n_grp, n_chip)),
        dma((n_grp, n_chip)),
        dma,
        dma,
        dma((n_chip,)),
        dma((n_chip,)),
        dma((n_grp,)),
        dma((n_grp,)),
    ]
    same, mixed = pl.pallas_call(
        functools.partial(kernel, n_grp, n_wide),
        out_shape=[jax.ShapeDtypeStruct(coeff.shape, F32)] * 2,
        in_specs=[pl.BlockSpec(memory_space=pltpu.HBM)] * len(operands),
        out_specs=[pl.BlockSpec(memory_space=pltpu.HBM)] * 2,
        scratch_shapes=scratch,
        compiler_params=pltpu.CompilerParams(
            collective_id=0, has_side_effects=True, vmem_limit_bytes=64 * 2**20 - 2**16
        ),
    )(*operands)
    return same + mixed


def suits(n_grp, n_wide, args):
    coeff, beta, _, _, _, source, _, _, occupation, _ = args
    rows, width = coeff.shape
    n_orb = occupation.shape[0]
    n_strings = n_grp * n_wide * rows
    return (
        n_grp > 1
        and n_wide > 2
        and n_wide % 8 == 0
        and rows == 8
        and width % (n_wide * LANES) == 0
        and beta.shape[1] == LANES
        and beta.shape[0] % (2 * n_wide // 2) == 0
        and beta.shape[0] <= LANES
        and width // LANES % 16 == 0
        and n_orb % 2 == 0
        and source.shape[0] <= LANES
        and source.shape[1] == LANES
        and n_wide * rows == LANES
        and n_strings % LANES == 0
        and n_strings <= 512
    )


def general(
    coeff,
    beta_blocks,
    block_list,
    alpha_blocks,
    partner_mask,
    exc_source,
    exc_pair,
    exc_parity,
    occupation,
    coulomb,
):
    alpha_rows, beta_width = coeff.shape
    block_size = beta_blocks.shape[1]
    block_count = beta_width // block_size
    blocked = coeff.reshape(alpha_rows, block_count, block_size)
    block_ids = jnp.arange(block_count, dtype=jnp.int32)
    choosing = (block_list[0][:, None] == block_ids[None, :]).astype(jnp.float32)
    picked = jnp.einsum("rnk,pn->rpk", blocked, choosing, precision=HIGH)
    applied = jnp.einsum("rpk,pkl->rpl", picked, beta_blocks, precision=HIGH)
    placing = (block_list[1][:, None] == block_ids[None, :]).astype(jnp.float32)
    same_beta = jnp.einsum("rpl,pn->rnl", applied, placing, precision=HIGH).reshape(
        alpha_rows, beta_width
    )
    masked = alpha_blocks[0] * partner_mask[0][:, None, None].astype(jnp.float32)
    group_count = masked.shape[0]
    coupling = masked.transpose(1, 0, 2).reshape(alpha_rows, group_count * alpha_rows)
    same_alpha = jnp.dot(
        coupling,
        lax.all_gather(coeff, "grp", axis=0, tiled=True),
        precision=HIGH,
        preferred_element_type=jnp.float32,
    )
    beta_major = lax.all_to_all(coeff, "wide", split_axis=1, concat_axis=0, tiled=True)
    every_string = lax.all_gather(beta_major, "grp", axis=0, tiled=True)
    group_rows, slice_width = beta_major.shape
    replace_count = exc_source.shape[0]
    weights_local = jnp.dot(
        coulomb, occupation.astype(jnp.float32), precision=HIGH, preferred_element_type=jnp.float32
    )
    phases = 1.0 - 2.0 * exc_parity.astype(jnp.float32)
    row_block = 256 if group_rows % 256 == 0 else group_rows
    turns = group_rows // row_block

    def one_block(entry):
        sources, pairs, signs = entry
        fetched = jnp.take(every_string, sources, axis=0)
        factor = jnp.take(weights_local, pairs, axis=0)
        return jnp.sum(signs[:, :, None] * factor * fetched, axis=1)

    mixed_local = lax.map(
        one_block,
        (
            exc_source.T.reshape(turns, row_block, replace_count),
            exc_pair.T.reshape(turns, row_block, replace_count),
            phases.T.reshape(turns, row_block, replace_count),
        ),
    ).reshape(group_rows, slice_width)
    mixed = lax.all_to_all(mixed_local, "wide", split_axis=0, concat_axis=1, tiled=True)
    return same_beta + same_alpha + mixed


def per_device(n_grp, n_wide, *args):
    if suits(n_grp, n_wide, args):
        return fused(n_grp, n_wide, args)
    return general(*args)


def solution(mesh):
    in_specs = (
        P(("grp", "wide"), None),
        P(),
        P(),
        P(("grp", "wide"), None, None, None),
        P(("grp", "wide"), None),
        P(None, "grp"),
        P(None, "grp"),
        P(None, "grp"),
        P(None, "wide"),
        P(),
    )
    out_specs = P(("grp", "wide"), None)
    return jax.shard_map(
        functools.partial(per_device, mesh.shape["grp"], mesh.shape["wide"]),
        mesh=mesh, in_specs=in_specs,
        out_specs=out_specs,
        check_vma=False,
    )
```

```python
import functools

import jax
import jax.numpy as jnp
from jax import lax
from jax.experimental import pallas as pl
from jax.experimental.pallas import tpu as pltpu
from jax.sharding import PartitionSpec as P

HIGH = lax.Precision.HIGHEST
LANES = 128
MESH = pl.DeviceIdType.MESH
F32 = jnp.float32
BF16 = jnp.bfloat16


def split_two(x):
    high = x.astype(BF16).astype(F32)
    return high, x - high


def split_narrow(x):
    high = x.astype(BF16)
    return high, (x - high.astype(F32)).astype(BF16)


def kernel(
    n_grp,
    n_wide,
    coeff_hbm,
    beta_hbm,
    blocks_hbm,
    alpha_hbm,
    mask_hbm,
    source_hbm,
    pair_hbm,
    parity_hbm,
    occupation_hbm,
    coulomb_hbm,
    same,
    mixed,
    coeff,
    dense,
    blocks,
    alpha,
    mask,
    source,
    pair,
    parity,
    occupation,
    coulomb,
    strings,
    strings_three,
    partner,
    staged,
    same_vmem,
    tiles,
    blocks_smem,
    applied,
    placed,
    padded,
    source_pad,
    pair_t,
    sign_t,
    coulomb_pad,
    table,
    occ,
    m_three,
    in_sem,
    out_sem,
    go_send,
    go_recv,
    relay_send,
    relay_recv,
    mate_send,
    mate_recv,
    occ_send,
    occ_recv,
    back_send,
    back_recv,
    partner_send,
    partner_recv,
):
    g = lax.axis_index("grp")
    w = lax.axis_index("wide")
    chip = w // 2
    core = lax.rem(w, 2)
    n_chip = n_wide // 2
    mate = (g, 2 * chip + 1 - core)
    rows, width = coeff.shape
    cut = width // n_chip
    exc = source.shape[0]
    n_orb, n_pair = coulomb.shape
    chunks = table.shape[0]
    n_strings = n_grp * n_wide * rows
    n_r = -(-n_orb // 4) * 8
    n_m = rows // 2 * n_r
    p_size, size = dense.shape[:2]
    n_blocks = width // size

    barrier = pltpu.get_barrier_semaphore()

    def greet(d, _):
        to = 2 * lax.rem(chip + d, n_chip) + core
        pl.semaphore_signal(barrier, inc=1, device_id=(g, to), device_id_type=MESH)
        return 0

    lax.fori_loop(1, n_chip, greet, 0)
    for h in range(1, n_grp):
        pl.semaphore_signal(
            barrier, inc=1, device_id=(lax.rem(g + h, n_grp), w), device_id_type=MESH
        )
    pl.semaphore_signal(barrier, inc=1, device_id=mate, device_id_type=MESH)

    fetches = [
        pltpu.make_async_copy(a, b, in_sem.at[i])
        for i, (a, b) in enumerate(
            (
                (pair_hbm, pair),
                (parity_hbm, parity),
                (source_hbm, source),
                (coulomb_hbm, coulomb),
                (occupation_hbm, occupation.at[core]),
                (coeff_hbm, coeff),
                (blocks_hbm, blocks),
                (alpha_hbm, alpha),
                (mask_hbm, mask),
                (beta_hbm, dense),
                (blocks_hbm, blocks_smem),
            )
        )
    ]
    for fetch in fetches:
        fetch.start()
    pl.semaphore_wait(barrier, n_chip - 1 + n_grp)

    def columns(j):
        return pl.ds(pl.multiple_of(j * cut, LANES), cut)

    def slot(d, h):
        group = lax.rem(g - h + n_grp, n_grp)
        return group * n_wide + 2 * lax.rem(chip - d + n_chip, n_chip) + core

    def go(d):
        to = lax.rem(chip + d, n_chip)
        return pltpu.make_async_remote_copy(
            src_ref=coeff_hbm.at[:, columns(to)],
            dst_ref=strings.at[g * n_wide + w],
            send_sem=go_send.at[d],
            recv_sem=go_recv.at[d],
            device_id=(g, 2 * to + core),
            device_id_type=MESH,
        )

    def relay(d, h):
        return pltpu.make_async_remote_copy(
            src_ref=strings.at[slot(d, 0)],
            dst_ref=strings.at[slot(d, 0)],
            send_sem=relay_send.at[h, d],
            recv_sem=relay_recv.at[h, d],
            device_id=(lax.rem(g + h, n_grp), w),
            device_id_type=MESH,
        )

    def to_mate(d, h):
        return pltpu.make_async_remote_copy(
            src_ref=strings.at[slot(d, h)],
            dst_ref=strings.at[slot(d, h)],
            send_sem=mate_send.at[h, d],
            recv_sem=mate_recv.at[h, d],
            device_id=mate,
            device_id_type=MESH,
        )

    occ_copy = pltpu.make_async_remote_copy(
        src_ref=occupation_hbm,
        dst_ref=occupation.at[core],
        send_sem=occ_send,
        recv_sem=occ_recv,
        device_id=mate,
        device_id_type=MESH,
    )

    def back(d):
        to = lax.rem(chip + d, n_chip)
        return pltpu.make_async_remote_copy(
            src_ref=staged.at[to],
            dst_ref=mixed.at[:, columns(chip)],
            send_sem=back_send.at[d],
            recv_sem=back_recv.at[d],
            device_id=(g, 2 * to + core),
            device_id_type=MESH,
        )

    def across(h):
        return pltpu.make_async_remote_copy(
            src_ref=coeff_hbm,
            dst_ref=partner.at[g],
            send_sem=partner_send.at[h],
            recv_sem=partner_recv.at[h],
            device_id=(lax.rem(g + h, n_grp), w),
            device_id_type=MESH,
        )

    def far_first(k):
        half = (k + 1) // 2
        return n_chip // 2 + half - 2 * half * lax.rem(k, 2)

    def start_go(k, _):
        go(far_first(k)).start()
        return 0

    lax.fori_loop(0, n_chip - 1, start_go, 0)
    occ_copy.start()

    padded[...] = jnp.zeros_like(padded)
    occ[...] = jnp.zeros_like(occ)
    table[...] = jnp.zeros_like(table)
    fetches[0].wait()
    padded[0:exc, :] = pair[...]
    pair_t[...] = padded[...].T
    fetches[1].wait()
    padded[0:exc, :] = 1 - 2 * parity[...]
    sign_t[...] = padded[...].T.astype(F32)
    source_pad[...] = jnp.zeros_like(source_pad)
    fetches[2].wait()
    source_pad[0:exc, :] = source[...]
    fetches[3].wait()
    coulomb_pad[...] = jnp.zeros_like(coulomb_pad)
    coulomb_pad[:, 0:n_pair] = coulomb[...]
    for q in range(2):
        for c in range(chunks):
            line = coulomb_pad[:, c * LANES : (c + 1) * LANES]
            table[c, pl.ds(q, n_orb, stride=2), :] = line
    fetches[5].wait()
    strings[g * n_wide + w] = coeff[:, columns(chip)]
    partner[g] = coeff[...]
    for h in range(1, n_grp):
        relay(0, h).start()
    to_mate(0, 0).start()

    def build(to):
        block = 2 * to + core
        at = pl.ds(pl.multiple_of(block * rows, rows), rows)
        sublane = lax.broadcasted_iota(jnp.int32, (rows, LANES), 0)
        odd = sublane - sublane // 2 * 2 == 1
        string = lax.broadcasted_iota(jnp.int32, (16, n_strings), 1)
        all_pairs = pair_t[at, :]
        all_signs = sign_t[at, :]

        def of_two(x, a):
            return jnp.where(
                odd,
                jnp.broadcast_to(x[a + 1 : a + 2, :], (rows, LANES)),
                jnp.broadcast_to(x[a : a + 1, :], (rows, LANES)),
            )

        found = []
        for a in range(0, rows, 2):
            hits = []
            for b in (a, a + 1):
                column = jnp.full((rows, LANES), block * rows + b, jnp.int32)
                for e in range(0, LANES, 16):
                    if e >= exc:
                        hits.append(jnp.zeros((16, n_strings), BF16))
                        continue
                    pieces = [
                        jnp.take_along_axis(
                            source_pad[e + f : e + f + rows, :],
                            column,
                            axis=1,
                            mode="promise_in_bounds",
                        )
                        for f in (0, 8)
                    ]
                    both = jnp.concatenate(pieces, axis=0)
                    full = jnp.concatenate([both] * (n_strings // LANES), axis=1)
                    hits.append(jnp.where(full == string, 1.0, 0.0).astype(BF16))
            pairs = of_two(all_pairs, a)
            signs = of_two(all_signs, a)
            which = pairs // LANES
            lane = pairs - which * LANES
            parts = [[], []]
            for r in range(0, n_r, rows):
                value = None
                for c in range(chunks):
                    got = jnp.take_along_axis(
                        table[c, r : r + rows, :],
                        lane,
                        axis=1,
                        mode="promise_in_bounds",
                    )
                    value = got if value is None else jnp.where(which == c, got, value)
                for part, half in zip(parts, split_two(value * signs)):
                    part.append(
                        jnp.concatenate(
                            [jnp.where(odd, 0.0, half), jnp.where(odd, half, 0.0)], axis=1
                        )
                    )
            left = jnp.concatenate(parts[0] + parts[1], axis=0).astype(BF16)
            m = jnp.dot(left, jnp.concatenate(hits, axis=0), preferred_element_type=F32)
            found.append(m[:n_r] + m[n_r:])
        return split_narrow(jnp.concatenate(found, axis=0))

    def build_and_pass(i, _):
        d = 2 * i
        for to, (high, low) in [(q, build(q)) for q in (d, d + 1)]:
            m_three[to, :, 0:n_strings] = high
            m_three[to, :, n_strings : 2 * n_strings] = low
            m_three[to, :, 2 * n_strings :] = high

        @pl.when(i > 0)
        def _():
            pass_on(d)

        pass_on(d + 1)
        return 0

    def pass_on(d):
        go(d).wait_recv()
        for h in range(1, n_grp):
            relay(d, h).start()
        to_mate(d, 0).start()

    lax.fori_loop(0, n_chip // 2, build_and_pass, 0)
    def pass_relayed(d, _):
        for h in range(1, n_grp):
            relay(d, h).wait_recv()
            to_mate(d, h).start()
        return 0

    lax.fori_loop(0, n_chip, pass_relayed, 0)
    for h in range(1, n_grp):
        across(h).start()

    fetches[4].wait()
    occ_copy.wait_recv()
    half = occupation.shape[2]
    for q in range(2):
        for r in range(2):
            for c in range(0, half, LANES):
                occ[(q * half + c) // LANES, pl.ds(r, n_orb, stride=2), :] = (
                    occupation[q, :, c : c + LANES].astype(F32)
                )

    def wait_mate(d, _):
        for h in range(n_grp):
            to_mate(d, h).wait_recv()
        return 0

    lax.fori_loop(0, n_chip, wait_mate, 0)
    high, low = split_narrow(strings[...].reshape(n_strings, cut))
    strings_three[0:n_strings, :] = high
    strings_three[n_strings : 2 * n_strings, :] = high
    strings_three[2 * n_strings :, :] = low

    def reduce_rows(y):
        sublane = lax.broadcasted_iota(jnp.int32, (rows, cut), 0)
        factor = [
            jnp.concatenate([occ[c, r : r + rows, :] for c in range(cut // LANES)], axis=1)
            for r in range(0, n_r, rows)
        ]
        total = None
        for p in range(rows // 2):
            z = y[p * n_r : p * n_r + rows] * factor[0]
            for r in range(rows, n_r, rows):
                z += y[p * n_r + r : p * n_r + r + rows] * factor[r // rows]
            z += pltpu.roll(z, 4, 0)
            z += pltpu.roll(z, 2, 0)
            total = z if total is None else jnp.where(sublane // 2 == p, z, total)
        return total

    def mix_two(i, _):
        ds = [far_first(2 * i), far_first(2 * i + 1)]
        tos = [lax.rem(chip + d, n_chip) for d in ds]
        y = jnp.dot(
            jnp.concatenate([m_three[to] for to in tos], axis=0),
            strings_three[...],
            preferred_element_type=F32,
        )
        for q in range(2):
            staged[tos[q]] = reduce_rows(y[q * n_m : (q + 1) * n_m])
        back(ds[0]).start()

        @pl.when(i < n_chip // 2 - 1)
        def _():
            back(ds[1]).start()

        return 0

    lax.fori_loop(0, n_chip // 2, mix_two, 0)
    own = pltpu.make_async_copy(staged.at[chip], mixed.at[:, columns(chip)], out_sem.at[0])
    own.start()

    fetches[10].wait()
    for t in range(n_blocks):
        tiles[t] = coeff[:, t * size : (t + 1) * size]
    fetches[9].wait()

    def pick(k):
        high, low = split_two(tiles[blocks_smem[0, k]])
        return [
            jnp.concatenate([high, high], axis=1),
            jnp.concatenate([low, jnp.zeros_like(low)], axis=1),
        ]

    share = p_size // n_chip

    def apply_dense(d, _):
        results = []
        for i in range(0, share, 2):
            k = d * share + i
            lhs = jnp.concatenate(pick(k) + pick(k + 1), axis=0).astype(BF16)
            h0, l0 = split_narrow(dense[k])
            h1, l1 = split_narrow(dense[k + 1])
            rhs = jnp.concatenate(
                [jnp.concatenate([h0, h1], axis=1), jnp.concatenate([l0, l1], axis=1)], axis=0
            )
            y = jnp.dot(lhs, rhs, preferred_element_type=F32)
            results.append(y[0:rows, :size] + y[rows : 2 * rows, :size])
            results.append(y[2 * rows : 3 * rows, size:] + y[3 * rows :, size:])
        for i, result in enumerate(results):
            applied[pl.ds(d * share + i, rows, stride=p_size), :] = result
        return 0

    lax.fori_loop(0, n_chip, apply_dense, 0)

    fetches[6].wait()
    place = jnp.where(
        lax.broadcasted_iota(jnp.int32, (n_blocks, p_size), 0)
        == jnp.broadcast_to(blocks[1:2, :], (n_blocks, p_size)),
        1.0,
        0.0,
    ).astype(BF16)
    place = jnp.concatenate([place, place], axis=1)
    for r in range(0, rows, 2):
        parts = [split_narrow(applied[q * p_size : (q + 1) * p_size, :]) for q in (r, r + 1)]
        both = jnp.concatenate(
            [jnp.concatenate([part[i] for part in parts], axis=1) for i in range(2)], axis=0
        )
        y = jnp.dot(place, both, preferred_element_type=F32)
        placed[pl.ds(r, n_blocks, stride=rows), :] = y[:, :size]
        placed[pl.ds(r + 1, n_blocks, stride=rows), :] = y[:, size:]

    fetches[7].wait()
    fetches[8].wait()
    factors = []
    for h in range(n_grp):
        block = alpha[0, h] * mask[0:1, h : h + 1].astype(F32)
        factors.append(
            [jnp.broadcast_to(block[:, s : s + 1], (rows, size)) for s in range(rows)]
        )
    for h in range(1, n_grp):
        across(h).wait_recv()

    def couple(i, _):
        for j in range(4):
            t = 4 * i + j
            at = pl.ds(pl.multiple_of(t * size, size), size)
            total = placed[pl.ds(pl.multiple_of(t * rows, rows), rows), :]
            for h in range(n_grp):
                c = partner[h, :, at]
                for s in range(rows):
                    total += factors[h][s] * jnp.broadcast_to(c[s : s + 1, :], (rows, size))
            same_vmem[:, at] = total
        return 0

    lax.fori_loop(0, n_blocks // 4, couple, 0)

    write = pltpu.make_async_copy(same_vmem, same, out_sem.at[1])
    write.start()

    def drain(d, _):
        go(d).wait_send()
        back(d).wait()
        return 0

    lax.fori_loop(1, n_chip, drain, 0)

    def drain_passed(d, _):
        to_mate(d, 0).wait_send()
        for h in range(1, n_grp):
            relay(d, h).wait_send()
            to_mate(d, h).wait_send()
        return 0

    lax.fori_loop(0, n_chip, drain_passed, 0)
    occ_copy.wait_send()
    for h in range(1, n_grp):
        across(h).wait_send()
    own.wait()
    write.wait()


def fused(n_grp, n_wide, args):
    coeff, beta, blocks, alpha, mask, source, pair, parity, occupation, coulomb = args
    coulomb = coulomb.T
    rows, width = coeff.shape
    n_chip = n_wide // 2
    cut = width // n_chip
    n_orb, n_pair = coulomb.shape
    n_r = -(-n_orb // 4) * 8
    n_m = rows // 2 * n_r
    n_strings = n_grp * n_wide * rows
    table_width = -(-n_pair // LANES) * LANES
    p_size, size = beta.shape[:2]
    operands = (coeff, beta, blocks, alpha, mask, source, pair, parity, occupation, coulomb)
    landing = [pltpu.VMEM(x.shape, x.dtype) for x in operands]
    landing[8] = pltpu.VMEM((2,) + occupation.shape, occupation.dtype)
    dma = pltpu.SemaphoreType.DMA
    scratch = landing + [
        pltpu.VMEM((n_grp * n_wide, rows, cut), F32),
        pltpu.VMEM((3 * n_strings, cut), BF16),
        pltpu.VMEM((n_grp, rows, width), F32),
        pltpu.VMEM((n_chip, rows, cut), F32),
        pltpu.VMEM((rows, width), F32),
        pltpu.VMEM((width // size, rows, size), F32),
        pltpu.SMEM(blocks.shape, blocks.dtype),
        pltpu.VMEM((rows * p_size, size), F32),
        pltpu.VMEM((width // size * rows, size), F32),
        pltpu.VMEM((LANES, LANES), jnp.int32),
        pltpu.VMEM((LANES, LANES), jnp.int32),
        pltpu.VMEM((LANES, LANES), jnp.int32),
        pltpu.VMEM((LANES, LANES), F32),
        pltpu.VMEM((n_orb, table_width), F32),
        pltpu.VMEM((table_width // LANES, n_r, LANES), F32),
        pltpu.VMEM((cut // LANES, n_r, LANES), F32),
        pltpu.VMEM((n_chip, n_m, 3 * n_strings), BF16),
        dma((len(operands) + 1,)),
        dma((2,)),
        dma((n_chip,)),
        dma((n_chip,)),
        dma((n_grp, n_chip)),
        dma((n_grp, n_chip)),
        dma((n_grp, n_chip)),
        dma((n_grp, n_chip)),
        dma,
        dma,
        dma((n_chip,)),
        dma((n_chip,)),
        dma((n_grp,)),
        dma((n_grp,)),
    ]
    same, mixed = pl.pallas_call(
        functools.partial(kernel, n_grp, n_wide),
        out_shape=[jax.ShapeDtypeStruct(coeff.shape, F32)] * 2,
        in_specs=[pl.BlockSpec(memory_space=pltpu.HBM)] * len(operands),
        out_specs=[pl.BlockSpec(memory_space=pltpu.HBM)] * 2,
        scratch_shapes=scratch,
        compiler_params=pltpu.CompilerParams(
            collective_id=0, has_side_effects=True, vmem_limit_bytes=64 * 2**20 - 2**16
        ),
    )(*operands)
    return same + mixed


def suits(n_grp, n_wide, args):
    coeff, beta, _, _, _, source, _, _, occupation, _ = args
    rows, width = coeff.shape
    n_orb = occupation.shape[0]
    n_strings = n_grp * n_wide * rows
    return (
        n_grp > 1
        and n_wide > 2
        and n_wide % 8 == 0
        and rows == 8
        and width % (n_wide * LANES) == 0
        and beta.shape[1] == LANES
        and beta.shape[0] % (2 * n_wide // 2) == 0
        and beta.shape[0] <= LANES
        and width // LANES % 16 == 0
        and n_orb % 2 == 0
        and source.shape[0] <= LANES
        and source.shape[1] == LANES
        and n_wide * rows == LANES
        and n_strings % LANES == 0
        and n_strings <= 512
    )


def general(
    coeff,
    beta_blocks,
    block_list,
    alpha_blocks,
    partner_mask,
    exc_source,
    exc_pair,
    exc_parity,
    occupation,
    coulomb,
):
    alpha_rows, beta_width = coeff.shape
    block_size = beta_blocks.shape[1]
    block_count = beta_width // block_size
    blocked = coeff.reshape(alpha_rows, block_count, block_size)
    block_ids = jnp.arange(block_count, dtype=jnp.int32)
    choosing = (block_list[0][:, None] == block_ids[None, :]).astype(jnp.float32)
    picked = jnp.einsum("rnk,pn->rpk", blocked, choosing, precision=HIGH)
    applied = jnp.einsum("rpk,pkl->rpl", picked, beta_blocks, precision=HIGH)
    placing = (block_list[1][:, None] == block_ids[None, :]).astype(jnp.float32)
    same_beta = jnp.einsum("rpl,pn->rnl", applied, placing, precision=HIGH).reshape(
        alpha_rows, beta_width
    )
    masked = alpha_blocks[0] * partner_mask[0][:, None, None].astype(jnp.float32)
    group_count = masked.shape[0]
    coupling = masked.transpose(1, 0, 2).reshape(alpha_rows, group_count * alpha_rows)
    same_alpha = jnp.dot(
        coupling,
        lax.all_gather(coeff, "grp", axis=0, tiled=True),
        precision=HIGH,
        preferred_element_type=jnp.float32,
    )
    beta_major = lax.all_to_all(coeff, "wide", split_axis=1, concat_axis=0, tiled=True)
    every_string = lax.all_gather(beta_major, "grp", axis=0, tiled=True)
    group_rows, slice_width = beta_major.shape
    replace_count = exc_source.shape[0]
    weights_local = jnp.dot(
        coulomb, occupation.astype(jnp.float32), precision=HIGH, preferred_element_type=jnp.float32
    )
    phases = 1.0 - 2.0 * exc_parity.astype(jnp.float32)
    row_block = 256 if group_rows % 256 == 0 else group_rows
    turns = group_rows // row_block

    def one_block(entry):
        sources, pairs, signs = entry
        fetched = jnp.take(every_string, sources, axis=0)
        factor = jnp.take(weights_local, pairs, axis=0)
        return jnp.sum(signs[:, :, None] * factor * fetched, axis=1)

    mixed_local = lax.map(
        one_block,
        (
            exc_source.T.reshape(turns, row_block, replace_count),
            exc_pair.T.reshape(turns, row_block, replace_count),
            phases.T.reshape(turns, row_block, replace_count),
        ),
    ).reshape(group_rows, slice_width)
    mixed = lax.all_to_all(mixed_local, "wide", split_axis=0, concat_axis=1, tiled=True)
    return same_beta + same_alpha + mixed


def per_device(n_grp, n_wide, *args):
    if suits(n_grp, n_wide, args):
        return fused(n_grp, n_wide, args)
    return general(*args)


def solution(mesh):
    in_specs = (
        P(("grp", "wide"), None),
        P(),
        P(),
        P(("grp", "wide"), None, None, None),
        P(("grp", "wide"), None),
        P(None, "grp"),
        P(None, "grp"),
        P(None, "grp"),
        P(None, "wide"),
        P(),
    )
    out_specs = P(("grp", "wide"), None)
    return jax.shard_map(
        functools.partial(per_device, mesh.shape["grp"], mesh.shape["wide"]),
        mesh=mesh, in_specs=in_specs,
        out_specs=out_specs,
        check_vma=False,
    )
```

```python
import functools

import jax
import jax.numpy as jnp
from jax import lax
from jax.experimental import pallas as pl
from jax.experimental.pallas import tpu as pltpu
from jax.sharding import PartitionSpec as P

HIGH = lax.Precision.HIGHEST
LANES = 128
MESH = pl.DeviceIdType.MESH
F32 = jnp.float32
BF16 = jnp.bfloat16


def split_two(x):
    high = x.astype(BF16).astype(F32)
    return high, x - high


def split_narrow(x):
    high = x.astype(BF16)
    return high, (x - high.astype(F32)).astype(BF16)


def kernel(
    n_grp,
    n_wide,
    coeff_hbm,
    beta_hbm,
    blocks_hbm,
    alpha_hbm,
    mask_hbm,
    source_hbm,
    pair_hbm,
    parity_hbm,
    occupation_hbm,
    coulomb_hbm,
    same,
    mixed,
    coeff,
    dense,
    blocks,
    alpha,
    mask,
    source,
    pair,
    parity,
    occupation,
    coulomb,
    strings,
    strings_three,
    partner,
    staged,
    same_vmem,
    tiles,
    blocks_smem,
    applied,
    placed,
    padded,
    source_pad,
    pair_t,
    sign_t,
    coulomb_pad,
    table,
    occ,
    m_three,
    in_sem,
    out_sem,
    go_send,
    go_recv,
    relay_send,
    relay_recv,
    mate_send,
    mate_recv,
    occ_send,
    occ_recv,
    back_send,
    back_recv,
    partner_send,
    partner_recv,
):
    g = lax.axis_index("grp")
    w = lax.axis_index("wide")
    chip = w // 2
    core = lax.rem(w, 2)
    n_chip = n_wide // 2
    mate = (g, 2 * chip + 1 - core)
    rows, width = coeff.shape
    cut = width // n_chip
    exc = source.shape[0]
    n_orb, n_pair = coulomb.shape
    chunks = table.shape[0]
    n_own = n_wide * rows
    n_strings = n_grp * n_own
    n_r = -(-n_orb // 4) * 8
    n_m = rows // 2 * n_r
    p_size, size = dense.shape[:2]
    n_blocks = width // size

    barrier = pltpu.get_barrier_semaphore()

    def greet(d, _):
        to = 2 * lax.rem(chip + d, n_chip) + core
        pl.semaphore_signal(barrier, inc=1, device_id=(g, to), device_id_type=MESH)
        return 0

    lax.fori_loop(1, n_chip, greet, 0)
    for h in range(1, n_grp):
        pl.semaphore_signal(
            barrier, inc=1, device_id=(lax.rem(g + h, n_grp), w), device_id_type=MESH
        )
    pl.semaphore_signal(barrier, inc=1, device_id=mate, device_id_type=MESH)

    fetches = [
        pltpu.make_async_copy(a, b, in_sem.at[i])
        for i, (a, b) in enumerate(
            (
                (pair_hbm, pair),
                (parity_hbm, parity),
                (source_hbm, source),
                (coulomb_hbm, coulomb),
                (occupation_hbm, occupation.at[core]),
                (coeff_hbm, coeff),
                (blocks_hbm, blocks),
                (alpha_hbm, alpha),
                (mask_hbm, mask),
                (beta_hbm, dense),
                (blocks_hbm, blocks_smem),
            )
        )
    ]
    for fetch in fetches:
        fetch.start()
    pl.semaphore_wait(barrier, n_chip - 1 + n_grp)

    def columns(j):
        return pl.ds(pl.multiple_of(j * cut, LANES), cut)

    def slot(d, h):
        return h * n_wide + 2 * lax.rem(chip - d + n_chip, n_chip) + core

    def go(d):
        to = lax.rem(chip + d, n_chip)
        return pltpu.make_async_remote_copy(
            src_ref=coeff_hbm.at[:, columns(to)],
            dst_ref=strings.at[w],
            send_sem=go_send.at[d],
            recv_sem=go_recv.at[d],
            device_id=(g, 2 * to + core),
            device_id_type=MESH,
        )

    def relay(d, h):
        return pltpu.make_async_remote_copy(
            src_ref=strings.at[slot(d, 0)],
            dst_ref=strings.at[slot(d, h)],
            send_sem=relay_send.at[h, d],
            recv_sem=relay_recv.at[h, d],
            device_id=(lax.rem(g + h, n_grp), w),
            device_id_type=MESH,
        )

    def to_mate(d, h):
        return pltpu.make_async_remote_copy(
            src_ref=strings.at[slot(d, h)],
            dst_ref=strings.at[slot(d, h)],
            send_sem=mate_send.at[h, d],
            recv_sem=mate_recv.at[h, d],
            device_id=mate,
            device_id_type=MESH,
        )

    occ_copy = pltpu.make_async_remote_copy(
        src_ref=occupation_hbm,
        dst_ref=occupation.at[core],
        send_sem=occ_send,
        recv_sem=occ_recv,
        device_id=mate,
        device_id_type=MESH,
    )

    def back(d):
        to = lax.rem(chip + d, n_chip)
        return pltpu.make_async_remote_copy(
            src_ref=staged.at[to],
            dst_ref=mixed.at[:, columns(chip)],
            send_sem=back_send.at[d],
            recv_sem=back_recv.at[d],
            device_id=(g, 2 * to + core),
            device_id_type=MESH,
        )

    def across(h):
        return pltpu.make_async_remote_copy(
            src_ref=coeff_hbm,
            dst_ref=partner.at[g],
            send_sem=partner_send.at[h],
            recv_sem=partner_recv.at[h],
            device_id=(lax.rem(g + h, n_grp), w),
            device_id_type=MESH,
        )

    def far_first(k):
        half = (k + 1) // 2
        return n_chip // 2 + half - 2 * half * lax.rem(k, 2)

    def start_go(k, _):
        go(far_first(k)).start()
        return 0

    lax.fori_loop(0, n_chip - 1, start_go, 0)
    occ_copy.start()

    padded[...] = jnp.zeros_like(padded)
    occ[...] = jnp.zeros_like(occ)
    table[...] = jnp.zeros_like(table)
    fetches[0].wait()
    padded[0:exc, :] = pair[...]
    pair_t[...] = padded[...].T
    fetches[1].wait()
    padded[0:exc, :] = 1 - 2 * parity[...]
    sign_t[...] = padded[...].T.astype(F32)
    source_pad[...] = jnp.zeros_like(source_pad)
    fetches[2].wait()
    group = source[...] // n_own
    before = lax.rem(g + n_grp - group, n_grp)
    source_pad[0:exc, :] = before * n_own + source[...] - group * n_own
    fetches[3].wait()
    coulomb_pad[...] = jnp.zeros_like(coulomb_pad)
    coulomb_pad[:, 0:n_pair] = coulomb[...]
    for q in range(2):
        for c in range(chunks):
            line = coulomb_pad[:, c * LANES : (c + 1) * LANES]
            table[c, pl.ds(q, n_orb, stride=2), :] = line
    fetches[5].wait()
    strings[w] = coeff[:, columns(chip)]
    partner[g] = coeff[...]
    for h in range(1, n_grp):
        relay(0, h).start()
    to_mate(0, 0).start()

    def build(to):
        block = 2 * to + core
        at = pl.ds(pl.multiple_of(block * rows, rows), rows)
        sublane = lax.broadcasted_iota(jnp.int32, (rows, LANES), 0)
        odd = sublane - sublane // 2 * 2 == 1
        string = lax.broadcasted_iota(jnp.int32, (16, n_strings), 1)
        all_pairs = pair_t[at, :]
        all_signs = sign_t[at, :]

        def of_two(x, a):
            return jnp.where(
                odd,
                jnp.broadcast_to(x[a + 1 : a + 2, :], (rows, LANES)),
                jnp.broadcast_to(x[a : a + 1, :], (rows, LANES)),
            )

        found = []
        for a in range(0, rows, 2):
            hits = []
            for b in (a, a + 1):
                column = jnp.full((rows, LANES), block * rows + b, jnp.int32)
                for e in range(0, LANES, 16):
                    if e >= exc:
                        hits.append(jnp.zeros((16, n_strings), BF16))
                        continue
                    pieces = [
                        jnp.take_along_axis(
                            source_pad[e + f : e + f + rows, :],
                            column,
                            axis=1,
                            mode="promise_in_bounds",
                        )
                        for f in (0, 8)
                    ]
                    both = jnp.concatenate(pieces, axis=0)
                    full = jnp.concatenate([both] * (n_strings // LANES), axis=1)
                    hits.append(jnp.where(full == string, 1.0, 0.0).astype(BF16))
            pairs = of_two(all_pairs, a)
            signs = of_two(all_signs, a)
            which = pairs // LANES
            lane = pairs - which * LANES
            parts = [[], []]
            for r in range(0, n_r, rows):
                value = None
                for c in range(chunks):
                    got = jnp.take_along_axis(
                        table[c, r : r + rows, :],
                        lane,
                        axis=1,
                        mode="promise_in_bounds",
                    )
                    value = got if value is None else jnp.where(which == c, got, value)
                for part, half in zip(parts, split_two(value * signs)):
                    part.append(
                        jnp.concatenate(
                            [jnp.where(odd, 0.0, half), jnp.where(odd, half, 0.0)], axis=1
                        )
                    )
            left = jnp.concatenate(parts[0] + parts[1], axis=0).astype(BF16)
            m = jnp.dot(left, jnp.concatenate(hits, axis=0), preferred_element_type=F32)
            found.append(m[:n_r] + m[n_r:])
        return split_narrow(jnp.concatenate(found, axis=0))

    def build_and_pass(i, _):
        d = 2 * i
        for to, (high, low) in [(q, build(q)) for q in (d, d + 1)]:
            for h in range(n_grp):
                own = slice(h * n_own, (h + 1) * n_own)
                at = 3 * h * n_own
                m_three[to, :, at : at + n_own] = high[:, own]
                m_three[to, :, at + n_own : at + 2 * n_own] = low[:, own]
                m_three[to, :, at + 2 * n_own : at + 3 * n_own] = high[:, own]

        @pl.when(i > 0)
        def _():
            pass_on(d)

        pass_on(d + 1)
        return 0

    def pass_on(d):
        go(d).wait_recv()
        for h in range(1, n_grp):
            relay(d, h).start()
        to_mate(d, 0).start()

    lax.fori_loop(0, n_chip // 2, build_and_pass, 0)
    fetches[4].wait()
    occ_copy.wait_recv()
    half = occupation.shape[2]
    for q in range(2):
        for r in range(2):
            for c in range(0, half, LANES):
                occ[(q * half + c) // LANES, pl.ds(r, n_orb, stride=2), :] = (
                    occupation[q, :, c : c + LANES].astype(F32)
                )

    def narrow(h):
        own = strings[h * n_wide : (h + 1) * n_wide].reshape(n_own, cut)
        high, low = split_narrow(own)
        at = 3 * h * n_own
        strings_three[at : at + n_own, :] = high
        strings_three[at + n_own : at + 2 * n_own, :] = high
        strings_three[at + 2 * n_own : at + 3 * n_own, :] = low

    def wait_mate(h):
        def wait(d, _):
            to_mate(d, h).wait_recv()
            return 0

        lax.fori_loop(0, n_chip, wait, 0)
        narrow(h)

    def reduce_rows(y):
        sublane = lax.broadcasted_iota(jnp.int32, (rows, cut), 0)
        factor = [
            jnp.concatenate([occ[c, r : r + rows, :] for c in range(cut // LANES)], axis=1)
            for r in range(0, n_r, rows)
        ]
        total = None
        for p in range(rows // 2):
            z = y[p * n_r : p * n_r + rows] * factor[0]
            for r in range(rows, n_r, rows):
                z += y[p * n_r + r : p * n_r + r + rows] * factor[r // rows]
            z += pltpu.roll(z, 4, 0)
            z += pltpu.roll(z, 2, 0)
            total = z if total is None else jnp.where(sublane // 2 == p, z, total)
        return total

    def mix(i, columns_of):
        ds = [far_first(2 * i), far_first(2 * i + 1)]
        tos = [lax.rem(chip + d, n_chip) for d in ds]
        y = jnp.dot(
            jnp.concatenate([m_three[to, :, columns_of] for to in tos], axis=0),
            strings_three[columns_of, :],
            preferred_element_type=F32,
        )
        return ds, tos, [reduce_rows(y[q * n_m : (q + 1) * n_m]) for q in range(2)]

    def mix_own(i, _):
        _, tos, sums = mix(i, slice(0, 3 * n_own))
        for to, total in zip(tos, sums):
            staged[to] = total
        for d in (2 * i, 2 * i + 1):
            for h in range(1, n_grp):
                relay(d, h).wait_recv()
                to_mate(d, h).start()
        return 0

    def mix_rest(i, _):
        ds, tos, sums = mix(i, slice(3 * n_own, 3 * n_strings))
        for to, total in zip(tos, sums):
            staged[to] += total
        back(ds[0]).start()

        @pl.when(i < n_chip // 2 - 1)
        def _():
            back(ds[1]).start()

        return 0

    wait_mate(0)
    lax.fori_loop(0, n_chip // 2, mix_own, 0)
    for h in range(1, n_grp):
        across(h).start()

    fetches[10].wait()
    for t in range(n_blocks):
        tiles[t] = coeff[:, t * size : (t + 1) * size]
    fetches[9].wait()

    def pick(k):
        high, low = split_two(tiles[blocks_smem[0, k]])
        return [
            jnp.concatenate([high, high], axis=1),
            jnp.concatenate([low, jnp.zeros_like(low)], axis=1),
        ]

    share = p_size // n_chip

    def apply_dense(d, _):
        results = []
        for i in range(0, share, 2):
            k = d * share + i
            lhs = jnp.concatenate(pick(k) + pick(k + 1), axis=0).astype(BF16)
            h0, l0 = split_narrow(dense[k])
            h1, l1 = split_narrow(dense[k + 1])
            rhs = jnp.concatenate(
                [jnp.concatenate([h0, h1], axis=1), jnp.concatenate([l0, l1], axis=1)], axis=0
            )
            y = jnp.dot(lhs, rhs, preferred_element_type=F32)
            results.append(y[0:rows, :size] + y[rows : 2 * rows, :size])
            results.append(y[2 * rows : 3 * rows, size:] + y[3 * rows :, size:])
        for i, result in enumerate(results):
            applied[pl.ds(d * share + i, rows, stride=p_size), :] = result
        return 0

    lax.fori_loop(0, n_chip // 2, apply_dense, 0)
    for h in range(1, n_grp):
        wait_mate(h)
    lax.fori_loop(0, n_chip // 2, mix_rest, 0)
    own = pltpu.make_async_copy(staged.at[chip], mixed.at[:, columns(chip)], out_sem.at[0])
    own.start()

    lax.fori_loop(n_chip // 2, n_chip, apply_dense, 0)

    fetches[6].wait()
    place = jnp.where(
        lax.broadcasted_iota(jnp.int32, (n_blocks, p_size), 0)
        == jnp.broadcast_to(blocks[1:2, :], (n_blocks, p_size)),
        1.0,
        0.0,
    ).astype(BF16)
    place = jnp.concatenate([place, place], axis=1)
    for r in range(0, rows, 2):
        parts = [split_narrow(applied[q * p_size : (q + 1) * p_size, :]) for q in (r, r + 1)]
        both = jnp.concatenate(
            [jnp.concatenate([part[i] for part in parts], axis=1) for i in range(2)], axis=0
        )
        y = jnp.dot(place, both, preferred_element_type=F32)
        placed[pl.ds(r, n_blocks, stride=rows), :] = y[:, :size]
        placed[pl.ds(r + 1, n_blocks, stride=rows), :] = y[:, size:]

    fetches[7].wait()
    fetches[8].wait()
    factors = []
    for h in range(n_grp):
        block = alpha[0, h] * mask[0:1, h : h + 1].astype(F32)
        factors.append(
            [jnp.broadcast_to(block[:, s : s + 1], (rows, size)) for s in range(rows)]
        )
    for h in range(1, n_grp):
        across(h).wait_recv()

    def couple(i, _):
        for j in range(4):
            t = 4 * i + j
            at = pl.ds(pl.multiple_of(t * size, size), size)
            total = placed[pl.ds(pl.multiple_of(t * rows, rows), rows), :]
            for h in range(n_grp):
                c = partner[h, :, at]
                for s in range(rows):
                    total += factors[h][s] * jnp.broadcast_to(c[s : s + 1, :], (rows, size))
            same_vmem[:, at] = total
        return 0

    lax.fori_loop(0, n_blocks // 4, couple, 0)

    write = pltpu.make_async_copy(same_vmem, same, out_sem.at[1])
    write.start()

    def drain(d, _):
        go(d).wait_send()
        back(d).wait()
        return 0

    lax.fori_loop(1, n_chip, drain, 0)

    def drain_passed(d, _):
        to_mate(d, 0).wait_send()
        for h in range(1, n_grp):
            relay(d, h).wait_send()
            to_mate(d, h).wait_send()
        return 0

    lax.fori_loop(0, n_chip, drain_passed, 0)
    occ_copy.wait_send()
    for h in range(1, n_grp):
        across(h).wait_send()
    own.wait()
    write.wait()


def fused(n_grp, n_wide, args):
    coeff, beta, blocks, alpha, mask, source, pair, parity, occupation, coulomb = args
    coulomb = coulomb.T
    rows, width = coeff.shape
    n_chip = n_wide // 2
    cut = width // n_chip
    n_orb, n_pair = coulomb.shape
    n_r = -(-n_orb // 4) * 8
    n_m = rows // 2 * n_r
    n_strings = n_grp * n_wide * rows
    table_width = -(-n_pair // LANES) * LANES
    p_size, size = beta.shape[:2]
    operands = (coeff, beta, blocks, alpha, mask, source, pair, parity, occupation, coulomb)
    landing = [pltpu.VMEM(x.shape, x.dtype) for x in operands]
    landing[8] = pltpu.VMEM((2,) + occupation.shape, occupation.dtype)
    dma = pltpu.SemaphoreType.DMA
    scratch = landing + [
        pltpu.VMEM((n_grp * n_wide, rows, cut), F32),
        pltpu.VMEM((3 * n_strings, cut), BF16),
        pltpu.VMEM((n_grp, rows, width), F32),
        pltpu.VMEM((n_chip, rows, cut), F32),
        pltpu.VMEM((rows, width), F32),
        pltpu.VMEM((width // size, rows, size), F32),
        pltpu.SMEM(blocks.shape, blocks.dtype),
        pltpu.VMEM((rows * p_size, size), F32),
        pltpu.VMEM((width // size * rows, size), F32),
        pltpu.VMEM((LANES, LANES), jnp.int32),
        pltpu.VMEM((LANES, LANES), jnp.int32),
        pltpu.VMEM((LANES, LANES), jnp.int32),
        pltpu.VMEM((LANES, LANES), F32),
        pltpu.VMEM((n_orb, table_width), F32),
        pltpu.VMEM((table_width // LANES, n_r, LANES), F32),
        pltpu.VMEM((cut // LANES, n_r, LANES), F32),
        pltpu.VMEM((n_chip, n_m, 3 * n_strings), BF16),
        dma((len(operands) + 1,)),
        dma((2,)),
        dma((n_chip,)),
        dma((n_chip,)),
        dma((n_grp, n_chip)),
        dma((n_grp, n_chip)),
        dma((n_grp, n_chip)),
        dma((n_grp, n_chip)),
        dma,
        dma,
        dma((n_chip,)),
        dma((n_chip,)),
        dma((n_grp,)),
        dma((n_grp,)),
    ]
    same, mixed = pl.pallas_call(
        functools.partial(kernel, n_grp, n_wide),
        out_shape=[jax.ShapeDtypeStruct(coeff.shape, F32)] * 2,
        in_specs=[pl.BlockSpec(memory_space=pltpu.HBM)] * len(operands),
        out_specs=[pl.BlockSpec(memory_space=pltpu.HBM)] * 2,
        scratch_shapes=scratch,
        compiler_params=pltpu.CompilerParams(
            collective_id=0, has_side_effects=True, vmem_limit_bytes=64 * 2**20 - 2**16
        ),
    )(*operands)
    return same + mixed


def suits(n_grp, n_wide, args):
    coeff, beta, _, _, _, source, _, _, occupation, _ = args
    rows, width = coeff.shape
    n_orb = occupation.shape[0]
    n_strings = n_grp * n_wide * rows
    return (
        n_grp > 1
        and n_wide > 2
        and n_wide % 8 == 0
        and rows == 8
        and width % (n_wide * LANES) == 0
        and beta.shape[1] == LANES
        and beta.shape[0] % (2 * n_wide // 2) == 0
        and beta.shape[0] <= LANES
        and width // LANES % 16 == 0
        and n_orb % 2 == 0
        and source.shape[0] <= LANES
        and source.shape[1] == LANES
        and n_wide * rows == LANES
        and n_strings % LANES == 0
        and n_strings <= 512
    )


def general(
    coeff,
    beta_blocks,
    block_list,
    alpha_blocks,
    partner_mask,
    exc_source,
    exc_pair,
    exc_parity,
    occupation,
    coulomb,
):
    alpha_rows, beta_width = coeff.shape
    block_size = beta_blocks.shape[1]
    block_count = beta_width // block_size
    blocked = coeff.reshape(alpha_rows, block_count, block_size)
    block_ids = jnp.arange(block_count, dtype=jnp.int32)
    choosing = (block_list[0][:, None] == block_ids[None, :]).astype(jnp.float32)
    picked = jnp.einsum("rnk,pn->rpk", blocked, choosing, precision=HIGH)
    applied = jnp.einsum("rpk,pkl->rpl", picked, beta_blocks, precision=HIGH)
    placing = (block_list[1][:, None] == block_ids[None, :]).astype(jnp.float32)
    same_beta = jnp.einsum("rpl,pn->rnl", applied, placing, precision=HIGH).reshape(
        alpha_rows, beta_width
    )
    masked = alpha_blocks[0] * partner_mask[0][:, None, None].astype(jnp.float32)
    group_count = masked.shape[0]
    coupling = masked.transpose(1, 0, 2).reshape(alpha_rows, group_count * alpha_rows)
    same_alpha = jnp.dot(
        coupling,
        lax.all_gather(coeff, "grp", axis=0, tiled=True),
        precision=HIGH,
        preferred_element_type=jnp.float32,
    )
    beta_major = lax.all_to_all(coeff, "wide", split_axis=1, concat_axis=0, tiled=True)
    every_string = lax.all_gather(beta_major, "grp", axis=0, tiled=True)
    group_rows, slice_width = beta_major.shape
    replace_count = exc_source.shape[0]
    weights_local = jnp.dot(
        coulomb, occupation.astype(jnp.float32), precision=HIGH, preferred_element_type=jnp.float32
    )
    phases = 1.0 - 2.0 * exc_parity.astype(jnp.float32)
    row_block = 256 if group_rows % 256 == 0 else group_rows
    turns = group_rows // row_block

    def one_block(entry):
        sources, pairs, signs = entry
        fetched = jnp.take(every_string, sources, axis=0)
        factor = jnp.take(weights_local, pairs, axis=0)
        return jnp.sum(signs[:, :, None] * factor * fetched, axis=1)

    mixed_local = lax.map(
        one_block,
        (
            exc_source.T.reshape(turns, row_block, replace_count),
            exc_pair.T.reshape(turns, row_block, replace_count),
            phases.T.reshape(turns, row_block, replace_count),
        ),
    ).reshape(group_rows, slice_width)
    mixed = lax.all_to_all(mixed_local, "wide", split_axis=0, concat_axis=1, tiled=True)
    return same_beta + same_alpha + mixed


def per_device(n_grp, n_wide, *args):
    if suits(n_grp, n_wide, args):
        return fused(n_grp, n_wide, args)
    return general(*args)


def solution(mesh):
    in_specs = (
        P(("grp", "wide"), None),
        P(),
        P(),
        P(("grp", "wide"), None, None, None),
        P(("grp", "wide"), None),
        P(None, "grp"),
        P(None, "grp"),
        P(None, "grp"),
        P(None, "wide"),
        P(),
    )
    out_specs = P(("grp", "wide"), None)
    return jax.shard_map(
        functools.partial(per_device, mesh.shape["grp"], mesh.shape["wide"]),
        mesh=mesh, in_specs=in_specs,
        out_specs=out_specs,
        check_vma=False,
    )
```

```python
import functools

import jax
import jax.numpy as jnp
from jax import lax
from jax.experimental import pallas as pl
from jax.experimental.pallas import tpu as pltpu
from jax.sharding import PartitionSpec as P

HIGH = lax.Precision.HIGHEST
LANES = 128
MESH = pl.DeviceIdType.MESH
F32 = jnp.float32
BF16 = jnp.bfloat16


def split_two(x):
    high = x.astype(BF16).astype(F32)
    return high, x - high


def split_narrow(x):
    high = x.astype(BF16)
    return high, (x - high.astype(F32)).astype(BF16)


def kernel(
    n_grp,
    n_wide,
    coeff_hbm,
    beta_hbm,
    blocks_hbm,
    alpha_hbm,
    mask_hbm,
    source_hbm,
    pair_hbm,
    parity_hbm,
    occupation_hbm,
    coulomb_hbm,
    same,
    mixed,
    coeff,
    dense,
    blocks,
    alpha,
    mask,
    source,
    pair,
    parity,
    occupation,
    coulomb,
    strings,
    strings_three,
    partner,
    staged,
    same_vmem,
    tiles,
    blocks_smem,
    applied,
    placed,
    padded,
    source_t,
    pair_t,
    sign_t,
    coulomb_pad,
    table,
    occ,
    m_three,
    in_sem,
    out_sem,
    go_send,
    go_recv,
    relay_send,
    relay_recv,
    mate_send,
    mate_recv,
    occ_send,
    occ_recv,
    back_send,
    back_recv,
    partner_send,
    partner_recv,
):
    g = lax.axis_index("grp")
    w = lax.axis_index("wide")
    chip = w // 2
    core = lax.rem(w, 2)
    n_chip = n_wide // 2
    mate = (g, 2 * chip + 1 - core)
    rows, width = coeff.shape
    cut = width // n_chip
    exc = source.shape[0]
    n_orb, n_pair = coulomb.shape
    chunks = table.shape[0]
    n_strings = n_grp * n_wide * rows
    n_r = -(-n_orb // 4) * 8
    n_m = rows // 2 * n_r
    p_size, size = dense.shape[:2]
    n_blocks = width // size

    barrier = pltpu.get_barrier_semaphore()

    def greet(d, _):
        to = 2 * lax.rem(chip + d, n_chip) + core
        pl.semaphore_signal(barrier, inc=1, device_id=(g, to), device_id_type=MESH)
        return 0

    lax.fori_loop(1, n_chip, greet, 0)
    for h in range(1, n_grp):
        pl.semaphore_signal(
            barrier, inc=1, device_id=(lax.rem(g + h, n_grp), w), device_id_type=MESH
        )
    pl.semaphore_signal(barrier, inc=1, device_id=mate, device_id_type=MESH)

    fetches = [
        pltpu.make_async_copy(a, b, in_sem.at[i])
        for i, (a, b) in enumerate(
            (
                (pair_hbm, pair),
                (parity_hbm, parity),
                (source_hbm, source),
                (coulomb_hbm, coulomb),
                (occupation_hbm, occupation.at[core]),
                (coeff_hbm, coeff),
                (blocks_hbm, blocks),
                (alpha_hbm, alpha),
                (mask_hbm, mask),
                (beta_hbm, dense),
                (blocks_hbm, blocks_smem),
            )
        )
    ]
    for fetch in fetches:
        fetch.start()
    pl.semaphore_wait(barrier, n_chip - 1 + n_grp)

    def columns(j):
        return pl.ds(pl.multiple_of(j * cut, LANES), cut)

    def slot(d, h):
        group = lax.rem(g - h + n_grp, n_grp)
        return group * n_wide + 2 * lax.rem(chip - d + n_chip, n_chip) + core

    def go(d):
        to = lax.rem(chip + d, n_chip)
        return pltpu.make_async_remote_copy(
            src_ref=coeff_hbm.at[:, columns(to)],
            dst_ref=strings.at[g * n_wide + w],
            send_sem=go_send.at[d],
            recv_sem=go_recv.at[d],
            device_id=(g, 2 * to + core),
            device_id_type=MESH,
        )

    def relay(d, h):
        return pltpu.make_async_remote_copy(
            src_ref=strings.at[slot(d, 0)],
            dst_ref=strings.at[slot(d, 0)],
            send_sem=relay_send.at[h, d],
            recv_sem=relay_recv.at[h, d],
            device_id=(lax.rem(g + h, n_grp), w),
            device_id_type=MESH,
        )

    def to_mate(d, h):
        return pltpu.make_async_remote_copy(
            src_ref=strings.at[slot(d, h)],
            dst_ref=strings.at[slot(d, h)],
            send_sem=mate_send.at[h, d],
            recv_sem=mate_recv.at[h, d],
            device_id=mate,
            device_id_type=MESH,
        )

    occ_copy = pltpu.make_async_remote_copy(
        src_ref=occupation_hbm,
        dst_ref=occupation.at[core],
        send_sem=occ_send,
        recv_sem=occ_recv,
        device_id=mate,
        device_id_type=MESH,
    )

    def back(d):
        to = lax.rem(chip + d, n_chip)
        return pltpu.make_async_remote_copy(
            src_ref=staged.at[to],
            dst_ref=mixed.at[:, columns(chip)],
            send_sem=back_send.at[d],
            recv_sem=back_recv.at[d],
            device_id=(g, 2 * to + core),
            device_id_type=MESH,
        )

    def across(h):
        return pltpu.make_async_remote_copy(
            src_ref=coeff_hbm,
            dst_ref=partner.at[g],
            send_sem=partner_send.at[h],
            recv_sem=partner_recv.at[h],
            device_id=(lax.rem(g + h, n_grp), w),
            device_id_type=MESH,
        )

    def start_go(d, _):
        go(d).start()
        return 0

    lax.fori_loop(1, n_chip, start_go, 0)
    occ_copy.start()

    padded[...] = jnp.zeros_like(padded)
    occ[...] = jnp.zeros_like(occ)
    table[...] = jnp.zeros_like(table)
    fetches[0].wait()
    padded[0:exc, :] = pair[...]
    pair_t[...] = padded[...].T
    fetches[1].wait()
    padded[0:exc, :] = 1 - 2 * parity[...]
    sign_t[...] = padded[...].T.astype(F32)
    fetches[2].wait()
    padded[0:exc, :] = source[...]
    source_t[...] = padded[...].T
    fetches[3].wait()
    coulomb_pad[...] = jnp.zeros_like(coulomb_pad)
    coulomb_pad[:, 0:n_pair] = coulomb[...]
    for q in range(2):
        for c in range(chunks):
            line = coulomb_pad[:, c * LANES : (c + 1) * LANES]
            table[c, pl.ds(q, n_orb, stride=2), :] = line
    fetches[5].wait()
    strings[g * n_wide + w] = coeff[:, columns(chip)]
    partner[g] = coeff[...]
    for h in range(1, n_grp):
        relay(0, h).start()
    to_mate(0, 0).start()

    def build(to):
        block = 2 * to + core
        at = pl.ds(pl.multiple_of(block * rows, rows), rows)
        sublane = lax.broadcasted_iota(jnp.int32, (rows, LANES), 0)
        odd = sublane - sublane // 2 * 2 == 1
        string = lax.broadcasted_iota(jnp.int32, (n_strings, LANES), 0)
        sources = source_t[at, :]
        all_pairs = pair_t[at, :]
        all_signs = sign_t[at, :]

        def of_two(x, a):
            return jnp.where(
                odd,
                jnp.broadcast_to(x[a + 1 : a + 2, :], (rows, LANES)),
                jnp.broadcast_to(x[a : a + 1, :], (rows, LANES)),
            )

        found = []
        for a in range(0, rows, 2):
            hits = [
                jnp.where(
                    string == jnp.broadcast_to(sources[b : b + 1, :], (n_strings, LANES)), 1.0, 0.0
                ).astype(BF16)
                for b in (a, a + 1)
            ]
            pairs = of_two(all_pairs, a)
            signs = of_two(all_signs, a)
            which = pairs // LANES
            lane = pairs - which * LANES
            parts = [[], []]
            for r in range(0, n_r, rows):
                value = None
                for c in range(chunks):
                    got = jnp.take_along_axis(
                        table[c, r : r + rows, :],
                        lane,
                        axis=1,
                        mode="promise_in_bounds",
                    )
                    value = got if value is None else jnp.where(which == c, got, value)
                for part, half in zip(parts, split_two(value * signs)):
                    part.append(
                        jnp.concatenate(
                            [jnp.where(odd, 0.0, half), jnp.where(odd, half, 0.0)], axis=1
                        )
                    )
            left = jnp.concatenate(parts[0] + parts[1], axis=0).astype(BF16)
            m = lax.dot_general(
                left,
                jnp.concatenate(hits, axis=1),
                (((1,), (1,)), ((), ())),
                preferred_element_type=F32,
            )
            found.append(m[:n_r] + m[n_r:])
        return split_narrow(jnp.concatenate(found, axis=0))

    def build_and_pass(i, _):
        d = 2 * i
        for to, (high, low) in [(q, build(q)) for q in (d, d + 1)]:
            m_three[to, :, 0:n_strings] = high
            m_three[to, :, n_strings : 2 * n_strings] = low
            m_three[to, :, 2 * n_strings :] = high

        @pl.when(i > 0)
        def _():
            pass_on(d)

        pass_on(d + 1)
        return 0

    def pass_on(d):
        go(d).wait_recv()
        for h in range(1, n_grp):
            relay(d, h).start()
        to_mate(d, 0).start()

    lax.fori_loop(0, n_chip // 2, build_and_pass, 0)
    for h in range(1, n_grp):
        across(h).start()

    fetches[10].wait()
    for t in range(n_blocks):
        tiles[t] = coeff[:, t * size : (t + 1) * size]
    fetches[9].wait()

    def pick(k):
        high, low = split_two(tiles[blocks_smem[0, k]])
        return [
            jnp.concatenate([high, high], axis=1),
            jnp.concatenate([low, jnp.zeros_like(low)], axis=1),
        ]

    share = p_size // n_chip

    def dense_and_pass(d, _):
        results = []
        for i in range(0, share, 2):
            k = d * share + i
            lhs = jnp.concatenate(pick(k) + pick(k + 1), axis=0).astype(BF16)
            h0, l0 = split_narrow(dense[k])
            h1, l1 = split_narrow(dense[k + 1])
            rhs = jnp.concatenate(
                [jnp.concatenate([h0, h1], axis=1), jnp.concatenate([l0, l1], axis=1)], axis=0
            )
            y = jnp.dot(lhs, rhs, preferred_element_type=F32)
            results.append(y[0:rows, :size] + y[rows : 2 * rows, :size])
            results.append(y[2 * rows : 3 * rows, size:] + y[3 * rows :, size:])
        for i, result in enumerate(results):
            applied[pl.ds(d * share + i, rows, stride=p_size), :] = result
        for h in range(1, n_grp):
            relay(d, h).wait_recv()
            to_mate(d, h).start()
        return 0

    lax.fori_loop(0, n_chip, dense_and_pass, 0)

    fetches[4].wait()
    occ_copy.wait_recv()
    half = occupation.shape[2]
    for q in range(2):
        for r in range(2):
            for c in range(0, half, LANES):
                occ[(q * half + c) // LANES, pl.ds(r, n_orb, stride=2), :] = (
                    occupation[q, :, c : c + LANES].astype(F32)
                )

    def wait_mate(d, _):
        for h in range(n_grp):
            to_mate(d, h).wait_recv()
        return 0

    lax.fori_loop(0, n_chip, wait_mate, 0)
    high, low = split_narrow(strings[...].reshape(n_strings, cut))
    strings_three[0:n_strings, :] = high
    strings_three[n_strings : 2 * n_strings, :] = high
    strings_three[2 * n_strings :, :] = low

    def reduce_rows(y):
        sublane = lax.broadcasted_iota(jnp.int32, (rows, cut), 0)
        factor = [
            jnp.concatenate([occ[c, r : r + rows, :] for c in range(cut // LANES)], axis=1)
            for r in range(0, n_r, rows)
        ]
        total = None
        for p in range(rows // 2):
            z = y[p * n_r : p * n_r + rows] * factor[0]
            for r in range(rows, n_r, rows):
                z += y[p * n_r + r : p * n_r + r + rows] * factor[r // rows]
            z += pltpu.roll(z, 4, 0)
            z += pltpu.roll(z, 2, 0)
            total = z if total is None else jnp.where(sublane // 2 == p, z, total)
        return total

    def mix_four(i, _):
        d = 4 * i + 1
        tos = [lax.rem(chip + d + q, n_chip) for q in range(4)]
        for q in (0, 2):
            y = jnp.dot(
                jnp.concatenate([m_three[to] for to in tos[q : q + 2]], axis=0),
                strings_three[...],
                preferred_element_type=F32,
            )
            staged[tos[q]] = reduce_rows(y[:n_m])
            staged[tos[q + 1]] = reduce_rows(y[n_m:])
        for q in range(3):
            back(d + q).start()

        @pl.when(d + 3 < n_chip)
        def _():
            back(d + 3).start()

        return 0

    lax.fori_loop(0, n_chip // 4, mix_four, 0)
    own = pltpu.make_async_copy(staged.at[chip], mixed.at[:, columns(chip)], out_sem.at[0])
    own.start()

    fetches[6].wait()
    place = jnp.where(
        lax.broadcasted_iota(jnp.int32, (n_blocks, p_size), 0)
        == jnp.broadcast_to(blocks[1:2, :], (n_blocks, p_size)),
        1.0,
        0.0,
    ).astype(BF16)
    place = jnp.concatenate([place, place], axis=1)
    for r in range(0, rows, 2):
        parts = [split_narrow(applied[q * p_size : (q + 1) * p_size, :]) for q in (r, r + 1)]
        both = jnp.concatenate(
            [jnp.concatenate([part[i] for part in parts], axis=1) for i in range(2)], axis=0
        )
        y = jnp.dot(place, both, preferred_element_type=F32)
        placed[pl.ds(r, n_blocks, stride=rows), :] = y[:, :size]
        placed[pl.ds(r + 1, n_blocks, stride=rows), :] = y[:, size:]

    fetches[7].wait()
    fetches[8].wait()
    factors = []
    for h in range(n_grp):
        block = alpha[0, h] * mask[0:1, h : h + 1].astype(F32)
        factors.append(
            [jnp.broadcast_to(block[:, s : s + 1], (rows, size)) for s in range(rows)]
        )
    for h in range(1, n_grp):
        across(h).wait_recv()

    def couple(i, _):
        for j in range(4):
            t = 4 * i + j
            at = pl.ds(pl.multiple_of(t * size, size), size)
            total = placed[pl.ds(pl.multiple_of(t * rows, rows), rows), :]
            for h in range(n_grp):
                c = partner[h, :, at]
                for s in range(rows):
                    total += factors[h][s] * jnp.broadcast_to(c[s : s + 1, :], (rows, size))
            same_vmem[:, at] = total
        return 0

    lax.fori_loop(0, n_blocks // 4, couple, 0)

    write = pltpu.make_async_copy(same_vmem, same, out_sem.at[1])
    write.start()

    def drain(d, _):
        go(d).wait_send()
        back(d).wait()
        return 0

    lax.fori_loop(1, n_chip, drain, 0)

    def drain_passed(d, _):
        to_mate(d, 0).wait_send()
        for h in range(1, n_grp):
            relay(d, h).wait_send()
            to_mate(d, h).wait_send()
        return 0

    lax.fori_loop(0, n_chip, drain_passed, 0)
    occ_copy.wait_send()
    for h in range(1, n_grp):
        across(h).wait_send()
    own.wait()
    write.wait()


def fused(n_grp, n_wide, args):
    coeff, beta, blocks, alpha, mask, source, pair, parity, occupation, coulomb = args
    coulomb = coulomb.T
    rows, width = coeff.shape
    n_chip = n_wide // 2
    cut = width // n_chip
    n_orb, n_pair = coulomb.shape
    n_r = -(-n_orb // 4) * 8
    n_m = rows // 2 * n_r
    n_strings = n_grp * n_wide * rows
    table_width = -(-n_pair // LANES) * LANES
    p_size, size = beta.shape[:2]
    operands = (coeff, beta, blocks, alpha, mask, source, pair, parity, occupation, coulomb)
    landing = [pltpu.VMEM(x.shape, x.dtype) for x in operands]
    landing[8] = pltpu.VMEM((2,) + occupation.shape, occupation.dtype)
    dma = pltpu.SemaphoreType.DMA
    scratch = landing + [
        pltpu.VMEM((n_grp * n_wide, rows, cut), F32),
        pltpu.VMEM((3 * n_strings, cut), BF16),
        pltpu.VMEM((n_grp, rows, width), F32),
        pltpu.VMEM((n_chip, rows, cut), F32),
        pltpu.VMEM((rows, width), F32),
        pltpu.VMEM((width // size, rows, size), F32),
        pltpu.SMEM(blocks.shape, blocks.dtype),
        pltpu.VMEM((rows * p_size, size), F32),
        pltpu.VMEM((width // size * rows, size), F32),
        pltpu.VMEM((LANES, LANES), jnp.int32),
        pltpu.VMEM((LANES, LANES), jnp.int32),
        pltpu.VMEM((LANES, LANES), jnp.int32),
        pltpu.VMEM((LANES, LANES), F32),
        pltpu.VMEM((n_orb, table_width), F32),
        pltpu.VMEM((table_width // LANES, n_r, LANES), F32),
        pltpu.VMEM((cut // LANES, n_r, LANES), F32),
        pltpu.VMEM((n_chip, n_m, 3 * n_strings), BF16),
        dma((len(operands) + 1,)),
        dma((2,)),
        dma((n_chip,)),
        dma((n_chip,)),
        dma((n_grp, n_chip)),
        dma((n_grp, n_chip)),
        dma((n_grp, n_chip)),
        dma((n_grp, n_chip)),
        dma,
        dma,
        dma((n_chip,)),
        dma((n_chip,)),
        dma((n_grp,)),
        dma((n_grp,)),
    ]
    same, mixed = pl.pallas_call(
        functools.partial(kernel, n_grp, n_wide),
        out_shape=[jax.ShapeDtypeStruct(coeff.shape, F32)] * 2,
        in_specs=[pl.BlockSpec(memory_space=pltpu.HBM)] * len(operands),
        out_specs=[pl.BlockSpec(memory_space=pltpu.HBM)] * 2,
        scratch_shapes=scratch,
        compiler_params=pltpu.CompilerParams(
            collective_id=0, has_side_effects=True, vmem_limit_bytes=64 * 2**20 - 2**16
        ),
    )(*operands)
    return same + mixed


def suits(n_grp, n_wide, args):
    coeff, beta, _, _, _, source, _, _, occupation, _ = args
    rows, width = coeff.shape
    n_orb = occupation.shape[0]
    n_strings = n_grp * n_wide * rows
    return (
        n_grp > 1
        and n_wide > 2
        and n_wide % 8 == 0
        and rows == 8
        and width % (n_wide * LANES) == 0
        and beta.shape[1] == LANES
        and beta.shape[0] % (2 * n_wide // 2) == 0
        and beta.shape[0] <= LANES
        and width // LANES % 16 == 0
        and n_orb % 2 == 0
        and source.shape[0] <= LANES
        and source.shape[1] == LANES
        and n_wide * rows == LANES
        and n_strings % LANES == 0
        and n_strings <= 512
    )


def general(
    coeff,
    beta_blocks,
    block_list,
    alpha_blocks,
    partner_mask,
    exc_source,
    exc_pair,
    exc_parity,
    occupation,
    coulomb,
):
    alpha_rows, beta_width = coeff.shape
    block_size = beta_blocks.shape[1]
    block_count = beta_width // block_size
    blocked = coeff.reshape(alpha_rows, block_count, block_size)
    block_ids = jnp.arange(block_count, dtype=jnp.int32)
    choosing = (block_list[0][:, None] == block_ids[None, :]).astype(jnp.float32)
    picked = jnp.einsum("rnk,pn->rpk", blocked, choosing, precision=HIGH)
    applied = jnp.einsum("rpk,pkl->rpl", picked, beta_blocks, precision=HIGH)
    placing = (block_list[1][:, None] == block_ids[None, :]).astype(jnp.float32)
    same_beta = jnp.einsum("rpl,pn->rnl", applied, placing, precision=HIGH).reshape(
        alpha_rows, beta_width
    )
    masked = alpha_blocks[0] * partner_mask[0][:, None, None].astype(jnp.float32)
    group_count = masked.shape[0]
    coupling = masked.transpose(1, 0, 2).reshape(alpha_rows, group_count * alpha_rows)
    same_alpha = jnp.dot(
        coupling,
        lax.all_gather(coeff, "grp", axis=0, tiled=True),
        precision=HIGH,
        preferred_element_type=jnp.float32,
    )
    beta_major = lax.all_to_all(coeff, "wide", split_axis=1, concat_axis=0, tiled=True)
    every_string = lax.all_gather(beta_major, "grp", axis=0, tiled=True)
    group_rows, slice_width = beta_major.shape
    replace_count = exc_source.shape[0]
    weights_local = jnp.dot(
        coulomb, occupation.astype(jnp.float32), precision=HIGH, preferred_element_type=jnp.float32
    )
    phases = 1.0 - 2.0 * exc_parity.astype(jnp.float32)
    row_block = 256 if group_rows % 256 == 0 else group_rows
    turns = group_rows // row_block

    def one_block(entry):
        sources, pairs, signs = entry
        fetched = jnp.take(every_string, sources, axis=0)
        factor = jnp.take(weights_local, pairs, axis=0)
        return jnp.sum(signs[:, :, None] * factor * fetched, axis=1)

    mixed_local = lax.map(
        one_block,
        (
            exc_source.T.reshape(turns, row_block, replace_count),
            exc_pair.T.reshape(turns, row_block, replace_count),
            phases.T.reshape(turns, row_block, replace_count),
        ),
    ).reshape(group_rows, slice_width)
    mixed = lax.all_to_all(mixed_local, "wide", split_axis=0, concat_axis=1, tiled=True)
    return same_beta + same_alpha + mixed


def per_device(n_grp, n_wide, *args):
    if suits(n_grp, n_wide, args):
        return fused(n_grp, n_wide, args)
    return general(*args)


def solution(mesh):
    in_specs = (
        P(("grp", "wide"), None),
        P(),
        P(),
        P(("grp", "wide"), None, None, None),
        P(("grp", "wide"), None),
        P(None, "grp"),
        P(None, "grp"),
        P(None, "grp"),
        P(None, "wide"),
        P(),
    )
    out_specs = P(("grp", "wide"), None)
    return jax.shard_map(
        functools.partial(per_device, mesh.shape["grp"], mesh.shape["wide"]),
        mesh=mesh, in_specs=in_specs,
        out_specs=out_specs,
        check_vma=False,
    )
```

```python
import functools

import jax
import jax.numpy as jnp
from jax import lax
from jax.experimental import pallas as pl
from jax.experimental.pallas import tpu as pltpu
from jax.sharding import PartitionSpec as P

HIGH = lax.Precision.HIGHEST
LANES = 128
MESH = pl.DeviceIdType.MESH
F32 = jnp.float32
BF16 = jnp.bfloat16


def split_two(x):
    high = x.astype(BF16).astype(F32)
    return high, x - high


def split_narrow(x):
    high = x.astype(BF16)
    return high, (x - high.astype(F32)).astype(BF16)


def kernel(
    n_grp,
    n_wide,
    coeff_hbm,
    beta_hbm,
    blocks_hbm,
    alpha_hbm,
    mask_hbm,
    source_hbm,
    pair_hbm,
    parity_hbm,
    occupation_hbm,
    coulomb_hbm,
    same,
    mixed,
    coeff,
    dense,
    blocks,
    alpha,
    mask,
    source,
    pair,
    parity,
    occupation,
    coulomb,
    strings,
    strings_three,
    partner,
    staged,
    same_vmem,
    tiles,
    blocks_smem,
    applied,
    placed,
    padded,
    source_t,
    pair_t,
    sign_t,
    coulomb_pad,
    table,
    occ,
    m_three,
    in_sem,
    out_sem,
    go_send,
    go_recv,
    relay_send,
    relay_recv,
    mate_send,
    mate_recv,
    occ_send,
    occ_recv,
    back_send,
    back_recv,
    partner_send,
    partner_recv,
):
    g = lax.axis_index("grp")
    w = lax.axis_index("wide")
    chip = w // 2
    core = lax.rem(w, 2)
    n_chip = n_wide // 2
    mate = (g, 2 * chip + 1 - core)
    rows, width = coeff.shape
    cut = width // n_chip
    exc = source.shape[0]
    n_orb, n_pair = coulomb.shape
    chunks = table.shape[0]
    n_strings = n_grp * n_wide * rows
    n_r = -(-n_orb // 4) * 8
    n_m = rows // 2 * n_r
    p_size, size = dense.shape[:2]
    n_blocks = width // size

    barrier = pltpu.get_barrier_semaphore()

    def greet(d, _):
        to = 2 * lax.rem(chip + d, n_chip) + core
        pl.semaphore_signal(barrier, inc=1, device_id=(g, to), device_id_type=MESH)
        return 0

    lax.fori_loop(1, n_chip, greet, 0)
    for h in range(1, n_grp):
        pl.semaphore_signal(
            barrier, inc=1, device_id=(lax.rem(g + h, n_grp), w), device_id_type=MESH
        )
    pl.semaphore_signal(barrier, inc=1, device_id=mate, device_id_type=MESH)

    fetches = [
        pltpu.make_async_copy(a, b, in_sem.at[i])
        for i, (a, b) in enumerate(
            (
                (pair_hbm, pair),
                (parity_hbm, parity),
                (source_hbm, source),
                (coulomb_hbm, coulomb),
                (occupation_hbm, occupation.at[core]),
                (coeff_hbm, coeff),
                (blocks_hbm, blocks),
                (alpha_hbm, alpha),
                (mask_hbm, mask),
                (beta_hbm, dense),
                (blocks_hbm, blocks_smem),
            )
        )
    ]
    for fetch in fetches:
        fetch.start()
    pl.semaphore_wait(barrier, n_chip - 1 + n_grp)

    def columns(j):
        return pl.ds(pl.multiple_of(j * cut, LANES), cut)

    def slot(d, h):
        group = lax.rem(g - h + n_grp, n_grp)
        return group * n_wide + 2 * lax.rem(chip - d + n_chip, n_chip) + core

    def go(d):
        to = lax.rem(chip + d, n_chip)
        return pltpu.make_async_remote_copy(
            src_ref=coeff_hbm.at[:, columns(to)],
            dst_ref=strings.at[g * n_wide + w],
            send_sem=go_send.at[d],
            recv_sem=go_recv.at[d],
            device_id=(g, 2 * to + core),
            device_id_type=MESH,
        )

    def relay(d, h):
        return pltpu.make_async_remote_copy(
            src_ref=strings.at[slot(d, 0)],
            dst_ref=strings.at[slot(d, 0)],
            send_sem=relay_send.at[h, d],
            recv_sem=relay_recv.at[h, d],
            device_id=(lax.rem(g + h, n_grp), w),
            device_id_type=MESH,
        )

    def to_mate(d, h):
        return pltpu.make_async_remote_copy(
            src_ref=strings.at[slot(d, h)],
            dst_ref=strings.at[slot(d, h)],
            send_sem=mate_send.at[h, d],
            recv_sem=mate_recv.at[h, d],
            device_id=mate,
            device_id_type=MESH,
        )

    occ_copy = pltpu.make_async_remote_copy(
        src_ref=occupation_hbm,
        dst_ref=occupation.at[core],
        send_sem=occ_send,
        recv_sem=occ_recv,
        device_id=mate,
        device_id_type=MESH,
    )

    def back(d):
        to = lax.rem(chip + d, n_chip)
        return pltpu.make_async_remote_copy(
            src_ref=staged.at[to],
            dst_ref=mixed.at[:, columns(chip)],
            send_sem=back_send.at[d],
            recv_sem=back_recv.at[d],
            device_id=(g, 2 * to + core),
            device_id_type=MESH,
        )

    def across(h):
        return pltpu.make_async_remote_copy(
            src_ref=coeff_hbm,
            dst_ref=partner.at[g],
            send_sem=partner_send.at[h],
            recv_sem=partner_recv.at[h],
            device_id=(lax.rem(g + h, n_grp), w),
            device_id_type=MESH,
        )

    def far_first(k):
        half = (k + 1) // 2
        return n_chip // 2 + half - 2 * half * lax.rem(k, 2)

    def start_go(k, _):
        go(far_first(k)).start()
        return 0

    lax.fori_loop(0, n_chip - 1, start_go, 0)
    occ_copy.start()

    padded[...] = jnp.zeros_like(padded)
    occ[...] = jnp.zeros_like(occ)
    table[...] = jnp.zeros_like(table)
    fetches[0].wait()
    padded[0:exc, :] = pair[...]
    pair_t[...] = padded[...].T
    fetches[1].wait()
    padded[0:exc, :] = 1 - 2 * parity[...]
    sign_t[...] = padded[...].T.astype(F32)
    fetches[2].wait()
    padded[0:exc, :] = source[...]
    source_t[...] = padded[...].T
    fetches[3].wait()
    coulomb_pad[...] = jnp.zeros_like(coulomb_pad)
    coulomb_pad[:, 0:n_pair] = coulomb[...]
    for q in range(2):
        for c in range(chunks):
            line = coulomb_pad[:, c * LANES : (c + 1) * LANES]
            table[c, pl.ds(q, n_orb, stride=2), :] = line
    fetches[5].wait()
    strings[g * n_wide + w] = coeff[:, columns(chip)]
    partner[g] = coeff[...]
    for h in range(1, n_grp):
        relay(0, h).start()
    to_mate(0, 0).start()

    def build(to):
        block = 2 * to + core
        at = pl.ds(pl.multiple_of(block * rows, rows), rows)
        sublane = lax.broadcasted_iota(jnp.int32, (rows, LANES), 0)
        odd = sublane - sublane // 2 * 2 == 1
        string = lax.broadcasted_iota(jnp.int32, (n_strings, LANES), 0)
        sources = source_t[at, :]
        all_pairs = pair_t[at, :]
        all_signs = sign_t[at, :]

        def of_two(x, a):
            return jnp.where(
                odd,
                jnp.broadcast_to(x[a + 1 : a + 2, :], (rows, LANES)),
                jnp.broadcast_to(x[a : a + 1, :], (rows, LANES)),
            )

        found = []
        for a in range(0, rows, 2):
            hits = [
                jnp.where(
                    string == jnp.broadcast_to(sources[b : b + 1, :], (n_strings, LANES)), 1.0, 0.0
                ).astype(BF16)
                for b in (a, a + 1)
            ]
            pairs = of_two(all_pairs, a)
            signs = of_two(all_signs, a)
            which = pairs // LANES
            lane = pairs - which * LANES
            parts = [[], []]
            for r in range(0, n_r, rows):
                value = None
                for c in range(chunks):
                    got = jnp.take_along_axis(
                        table[c, r : r + rows, :],
                        lane,
                        axis=1,
                        mode="promise_in_bounds",
                    )
                    value = got if value is None else jnp.where(which == c, got, value)
                for part, half in zip(parts, split_two(value * signs)):
                    part.append(
                        jnp.concatenate(
                            [jnp.where(odd, 0.0, half), jnp.where(odd, half, 0.0)], axis=1
                        )
                    )
            left = jnp.concatenate(parts[0] + parts[1], axis=0).astype(BF16)
            m = lax.dot_general(
                left,
                jnp.concatenate(hits, axis=1),
                (((1,), (1,)), ((), ())),
                preferred_element_type=F32,
            )
            found.append(m[:n_r] + m[n_r:])
        return split_narrow(jnp.concatenate(found, axis=0))

    def build_and_pass(i, _):
        d = 2 * i
        for to, (high, low) in [(q, build(q)) for q in (d, d + 1)]:
            m_three[to, :, 0:n_strings] = high
            m_three[to, :, n_strings : 2 * n_strings] = low
            m_three[to, :, 2 * n_strings :] = high

        @pl.when(i > 0)
        def _():
            pass_on(d)

        pass_on(d + 1)
        return 0

    def pass_on(d):
        go(d).wait_recv()
        for h in range(1, n_grp):
            relay(d, h).start()
        to_mate(d, 0).start()

    lax.fori_loop(0, n_chip // 2, build_and_pass, 0)

    fetches[10].wait()
    for t in range(n_blocks):
        tiles[t] = coeff[:, t * size : (t + 1) * size]
    fetches[9].wait()

    def pick(k):
        high, low = split_two(tiles[blocks_smem[0, k]])
        return [
            jnp.concatenate([high, high], axis=1),
            jnp.concatenate([low, jnp.zeros_like(low)], axis=1),
        ]

    share = p_size // n_chip

    def dense_and_pass(d, _):
        results = []
        for i in range(0, share, 2):
            k = d * share + i
            lhs = jnp.concatenate(pick(k) + pick(k + 1), axis=0).astype(BF16)
            h0, l0 = split_narrow(dense[k])
            h1, l1 = split_narrow(dense[k + 1])
            rhs = jnp.concatenate(
                [jnp.concatenate([h0, h1], axis=1), jnp.concatenate([l0, l1], axis=1)], axis=0
            )
            y = jnp.dot(lhs, rhs, preferred_element_type=F32)
            results.append(y[0:rows, :size] + y[rows : 2 * rows, :size])
            results.append(y[2 * rows : 3 * rows, size:] + y[3 * rows :, size:])
        for i, result in enumerate(results):
            applied[pl.ds(d * share + i, rows, stride=p_size), :] = result
        for h in range(1, n_grp):
            relay(d, h).wait_recv()
            to_mate(d, h).start()
        return 0

    lax.fori_loop(0, n_chip, dense_and_pass, 0)
    for h in range(1, n_grp):
        across(h).start()

    fetches[4].wait()
    occ_copy.wait_recv()
    half = occupation.shape[2]
    for q in range(2):
        for r in range(2):
            for c in range(0, half, LANES):
                occ[(q * half + c) // LANES, pl.ds(r, n_orb, stride=2), :] = (
                    occupation[q, :, c : c + LANES].astype(F32)
                )

    def wait_mate(d, _):
        for h in range(n_grp):
            to_mate(d, h).wait_recv()
        return 0

    lax.fori_loop(0, n_chip, wait_mate, 0)
    high, low = split_narrow(strings[...].reshape(n_strings, cut))
    strings_three[0:n_strings, :] = high
    strings_three[n_strings : 2 * n_strings, :] = high
    strings_three[2 * n_strings :, :] = low

    def reduce_rows(y):
        sublane = lax.broadcasted_iota(jnp.int32, (rows, cut), 0)
        factor = [
            jnp.concatenate([occ[c, r : r + rows, :] for c in range(cut // LANES)], axis=1)
            for r in range(0, n_r, rows)
        ]
        total = None
        for p in range(rows // 2):
            z = y[p * n_r : p * n_r + rows] * factor[0]
            for r in range(rows, n_r, rows):
                z += y[p * n_r + r : p * n_r + r + rows] * factor[r // rows]
            z += pltpu.roll(z, 4, 0)
            z += pltpu.roll(z, 2, 0)
            total = z if total is None else jnp.where(sublane // 2 == p, z, total)
        return total

    def mix_two(i, _):
        ds = [far_first(2 * i), far_first(2 * i + 1)]
        tos = [lax.rem(chip + d, n_chip) for d in ds]
        y = jnp.dot(
            jnp.concatenate([m_three[to] for to in tos], axis=0),
            strings_three[...],
            preferred_element_type=F32,
        )
        for q in range(2):
            staged[tos[q]] = reduce_rows(y[q * n_m : (q + 1) * n_m])
        back(ds[0]).start()

        @pl.when(i < n_chip // 2 - 1)
        def _():
            back(ds[1]).start()

        return 0

    lax.fori_loop(0, n_chip // 2, mix_two, 0)
    own = pltpu.make_async_copy(staged.at[chip], mixed.at[:, columns(chip)], out_sem.at[0])
    own.start()

    fetches[6].wait()
    place = jnp.where(
        lax.broadcasted_iota(jnp.int32, (n_blocks, p_size), 0)
        == jnp.broadcast_to(blocks[1:2, :], (n_blocks, p_size)),
        1.0,
        0.0,
    ).astype(BF16)
    place = jnp.concatenate([place, place], axis=1)
    for r in range(0, rows, 2):
        parts = [split_narrow(applied[q * p_size : (q + 1) * p_size, :]) for q in (r, r + 1)]
        both = jnp.concatenate(
            [jnp.concatenate([part[i] for part in parts], axis=1) for i in range(2)], axis=0
        )
        y = jnp.dot(place, both, preferred_element_type=F32)
        placed[pl.ds(r, n_blocks, stride=rows), :] = y[:, :size]
        placed[pl.ds(r + 1, n_blocks, stride=rows), :] = y[:, size:]

    fetches[7].wait()
    fetches[8].wait()
    factors = []
    for h in range(n_grp):
        block = alpha[0, h] * mask[0:1, h : h + 1].astype(F32)
        factors.append(
            [jnp.broadcast_to(block[:, s : s + 1], (rows, size)) for s in range(rows)]
        )
    for h in range(1, n_grp):
        across(h).wait_recv()

    def couple(i, _):
        for j in range(4):
            t = 4 * i + j
            at = pl.ds(pl.multiple_of(t * size, size), size)
            total = placed[pl.ds(pl.multiple_of(t * rows, rows), rows), :]
            for h in range(n_grp):
                for s in range(rows):
                    total += factors[h][s] * jnp.broadcast_to(partner[h, s : s + 1, at], (rows, size))
            same_vmem[:, at] = total
        return 0

    lax.fori_loop(0, n_blocks // 4, couple, 0)

    write = pltpu.make_async_copy(same_vmem, same, out_sem.at[1])
    write.start()

    def drain(d, _):
        go(d).wait_send()
        back(d).wait()
        return 0

    lax.fori_loop(1, n_chip, drain, 0)

    def drain_passed(d, _):
        to_mate(d, 0).wait_send()
        for h in range(1, n_grp):
            relay(d, h).wait_send()
            to_mate(d, h).wait_send()
        return 0

    lax.fori_loop(0, n_chip, drain_passed, 0)
    occ_copy.wait_send()
    for h in range(1, n_grp):
        across(h).wait_send()
    own.wait()
    write.wait()


def fused(n_grp, n_wide, args):
    coeff, beta, blocks, alpha, mask, source, pair, parity, occupation, coulomb = args
    coulomb = coulomb.T
    rows, width = coeff.shape
    n_chip = n_wide // 2
    cut = width // n_chip
    n_orb, n_pair = coulomb.shape
    n_r = -(-n_orb // 4) * 8
    n_m = rows // 2 * n_r
    n_strings = n_grp * n_wide * rows
    table_width = -(-n_pair // LANES) * LANES
    p_size, size = beta.shape[:2]
    operands = (coeff, beta, blocks, alpha, mask, source, pair, parity, occupation, coulomb)
    landing = [pltpu.VMEM(x.shape, x.dtype) for x in operands]
    landing[8] = pltpu.VMEM((2,) + occupation.shape, occupation.dtype)
    dma = pltpu.SemaphoreType.DMA
    scratch = landing + [
        pltpu.VMEM((n_grp * n_wide, rows, cut), F32),
        pltpu.VMEM((3 * n_strings, cut), BF16),
        pltpu.VMEM((n_grp, rows, width), F32),
        pltpu.VMEM((n_chip, rows, cut), F32),
        pltpu.VMEM((rows, width), F32),
        pltpu.VMEM((width // size, rows, size), F32),
        pltpu.SMEM(blocks.shape, blocks.dtype),
        pltpu.VMEM((rows * p_size, size), F32),
        pltpu.VMEM((width // size * rows, size), F32),
        pltpu.VMEM((LANES, LANES), jnp.int32),
        pltpu.VMEM((LANES, LANES), jnp.int32),
        pltpu.VMEM((LANES, LANES), jnp.int32),
        pltpu.VMEM((LANES, LANES), F32),
        pltpu.VMEM((n_orb, table_width), F32),
        pltpu.VMEM((table_width // LANES, n_r, LANES), F32),
        pltpu.VMEM((cut // LANES, n_r, LANES), F32),
        pltpu.VMEM((n_chip, n_m, 3 * n_strings), BF16),
        dma((len(operands) + 1,)),
        dma((2,)),
        dma((n_chip,)),
        dma((n_chip,)),
        dma((n_grp, n_chip)),
        dma((n_grp, n_chip)),
        dma((n_grp, n_chip)),
        dma((n_grp, n_chip)),
        dma,
        dma,
        dma((n_chip,)),
        dma((n_chip,)),
        dma((n_grp,)),
        dma((n_grp,)),
    ]
    same, mixed = pl.pallas_call(
        functools.partial(kernel, n_grp, n_wide),
        out_shape=[jax.ShapeDtypeStruct(coeff.shape, F32)] * 2,
        in_specs=[pl.BlockSpec(memory_space=pltpu.HBM)] * len(operands),
        out_specs=[pl.BlockSpec(memory_space=pltpu.HBM)] * 2,
        scratch_shapes=scratch,
        compiler_params=pltpu.CompilerParams(
            collective_id=0, has_side_effects=True, vmem_limit_bytes=64 * 2**20 - 2**16
        ),
    )(*operands)
    return same + mixed


def suits(n_grp, n_wide, args):
    coeff, beta, _, _, _, source, _, _, occupation, _ = args
    rows, width = coeff.shape
    n_orb = occupation.shape[0]
    n_strings = n_grp * n_wide * rows
    return (
        n_grp > 1
        and n_wide > 2
        and n_wide % 8 == 0
        and rows == 8
        and width % (n_wide * LANES) == 0
        and beta.shape[1] == LANES
        and beta.shape[0] % (2 * n_wide // 2) == 0
        and beta.shape[0] <= LANES
        and width // LANES % 16 == 0
        and n_orb % 2 == 0
        and source.shape[0] <= LANES
        and source.shape[1] == LANES
        and n_wide * rows == LANES
        and n_strings % LANES == 0
        and n_strings <= 512
    )


def general(
    coeff,
    beta_blocks,
    block_list,
    alpha_blocks,
    partner_mask,
    exc_source,
    exc_pair,
    exc_parity,
    occupation,
    coulomb,
):
    alpha_rows, beta_width = coeff.shape
    block_size = beta_blocks.shape[1]
    block_count = beta_width // block_size
    blocked = coeff.reshape(alpha_rows, block_count, block_size)
    block_ids = jnp.arange(block_count, dtype=jnp.int32)
    choosing = (block_list[0][:, None] == block_ids[None, :]).astype(jnp.float32)
    picked = jnp.einsum("rnk,pn->rpk", blocked, choosing, precision=HIGH)
    applied = jnp.einsum("rpk,pkl->rpl", picked, beta_blocks, precision=HIGH)
    placing = (block_list[1][:, None] == block_ids[None, :]).astype(jnp.float32)
    same_beta = jnp.einsum("rpl,pn->rnl", applied, placing, precision=HIGH).reshape(
        alpha_rows, beta_width
    )
    masked = alpha_blocks[0] * partner_mask[0][:, None, None].astype(jnp.float32)
    group_count = masked.shape[0]
    coupling = masked.transpose(1, 0, 2).reshape(alpha_rows, group_count * alpha_rows)
    same_alpha = jnp.dot(
        coupling,
        lax.all_gather(coeff, "grp", axis=0, tiled=True),
        precision=HIGH,
        preferred_element_type=jnp.float32,
    )
    beta_major = lax.all_to_all(coeff, "wide", split_axis=1, concat_axis=0, tiled=True)
    every_string = lax.all_gather(beta_major, "grp", axis=0, tiled=True)
    group_rows, slice_width = beta_major.shape
    replace_count = exc_source.shape[0]
    weights_local = jnp.dot(
        coulomb, occupation.astype(jnp.float32), precision=HIGH, preferred_element_type=jnp.float32
    )
    phases = 1.0 - 2.0 * exc_parity.astype(jnp.float32)
    row_block = 256 if group_rows % 256 == 0 else group_rows
    turns = group_rows // row_block

    def one_block(entry):
        sources, pairs, signs = entry
        fetched = jnp.take(every_string, sources, axis=0)
        factor = jnp.take(weights_local, pairs, axis=0)
        return jnp.sum(signs[:, :, None] * factor * fetched, axis=1)

    mixed_local = lax.map(
        one_block,
        (
            exc_source.T.reshape(turns, row_block, replace_count),
            exc_pair.T.reshape(turns, row_block, replace_count),
            phases.T.reshape(turns, row_block, replace_count),
        ),
    ).reshape(group_rows, slice_width)
    mixed = lax.all_to_all(mixed_local, "wide", split_axis=0, concat_axis=1, tiled=True)
    return same_beta + same_alpha + mixed


def per_device(n_grp, n_wide, *args):
    if suits(n_grp, n_wide, args):
        return fused(n_grp, n_wide, args)
    return general(*args)


def solution(mesh):
    in_specs = (
        P(("grp", "wide"), None),
        P(),
        P(),
        P(("grp", "wide"), None, None, None),
        P(("grp", "wide"), None),
        P(None, "grp"),
        P(None, "grp"),
        P(None, "grp"),
        P(None, "wide"),
        P(),
    )
    out_specs = P(("grp", "wide"), None)
    return jax.shard_map(
        functools.partial(per_device, mesh.shape["grp"], mesh.shape["wide"]),
        mesh=mesh, in_specs=in_specs,
        out_specs=out_specs,
        check_vma=False,
    )
```
